32 devices in a mesh: grp: 4 (over y, x), tp: 8 (over z, core).
Axes of the slice: x: 2, y: 2, z: 4, core: 2. Of those that a mesh axis runs over, the one named last changes fastest.
Arguments:
- features: bfloat16 [1024, 49152], P('grp', 'tp'), may hold values from -24 to 24
- weight: bfloat16 [49152, 8192], P('tp', 'grp'), may hold values from -0.049804688 to 0.049804688
- norm_gain: float32 [8192], P('grp'), may hold values from 0.1 to 1.9
- target: bfloat16 [1024, 8192], P(None, 'grp'), may hold values from -6 to 6
- counts: int32 [128], replicated, may hold values from 1 to 8
Outputs:
- weight_grad: bfloat16 [49152, 8192], P('tp', 'grp')
- draft_loss: float32 [], replicated
The draws below stay inside these ranges and needn't reach their ends.
All inputs are finite; a program needn't handle non-finite values.
Results may differ from the reference program's by a relative error of at most 0.0085.
Values may be sent and summed in bfloat16 or wider, within the bound.
No kernel may reach another device: no remote copies, remote signals or barrier semaphores. Data moves between devices by JAX's collectives and lax.ppermute only.
A program may use at most 192 MiB of HBM per device.

```python
import math
import jax
import jax.numpy as jnp
from jax import lax

DM = 16384
DOUT = 8192
SPEC = 8
REQ = 32
TOKENS = 1024
N_GRP = 4


def draw_features(key, part):
    first, second, third = jax.random.split(key, 3)
    base = jax.random.normal(first, (TOKENS, 3 * DM), jnp.float32)
    base = jnp.clip(base, -4.0, 4.0)
    row_scale = jnp.exp(jax.random.uniform(second, (TOKENS, 1), jnp.float32, math.log(0.3), math.log(3.0)))
    col_scale = jnp.exp(jax.random.uniform(third, (1, 3 * DM), jnp.float32, math.log(0.5), math.log(2.0)))
    return jnp.clip(base * row_scale * col_scale, -24.0, 24.0).astype(jnp.bfloat16)


def draw_weight(key, part):
    first, second = jax.random.split(key, 2)
    base = jnp.clip(jax.random.normal(first, (3 * DM, DOUT), jnp.float32), -4.0, 4.0)
    col_scale = jnp.exp(jax.random.uniform(second, (1, DOUT), jnp.float32, math.log(0.3), math.log(3.0)))
    return jnp.clip(base * col_scale / math.sqrt(3 * DM), -0.0498046875, 0.0498046875).astype(jnp.bfloat16)


def plant(values, stream_key, least, top_value):
    dims = values.shape
    place = [jax.random.randint(jax.random.fold_in(stream_key, axis), (), 0, dims[axis]) for axis in range(len(dims))]
    values = values.at[tuple(place)].set(least)
    longest = dims.index(max(dims))
    place[longest] = (place[longest] + 1) % dims[longest]
    return values.at[tuple(place)].set(top_value)


def block_levels(rng, extent, pieces, low, largest):
    level, own = 1.0, jax.random.fold_in(rng, 6)
    for position, shards_of in pieces:
        draws = jnp.exp(jax.random.uniform(jax.random.fold_in(own, position), (shards_of,), jnp.float32, low / len(pieces), largest / len(pieces)))
        level = level * jnp.repeat(draws, extent[position] // shards_of).reshape([-1 if axis == position else 1 for axis in range(len(extent))])
    return level


def bell_draw(own_key, shape, scale, most, pieces=(), held_as=jnp.bfloat16):
    result = scale * jax.random.normal(own_key, shape, jnp.float32)
    if pieces:
        result = result * block_levels(own_key, shape, pieces, -0.22, 0.18)
    return jnp.clip(result, -most, most).astype(held_as)


def setup_inputs(seed: int = 0) -> dict:
    streams_of = jax.random.split(jax.random.key(seed), 6)
    return {
        "features": draw_features(jax.random.fold_in(streams_of[5], 71), 0),
        "weight": draw_weight(jax.random.fold_in(streams_of[5], 71), 0),
        "norm_gain": jnp.clip(1.0 + 0.18 * jax.random.normal(streams_of[2], (DOUT,), jnp.float32), 0.1, 1.9),
        "target": bell_draw(streams_of[3], (TOKENS, DOUT), 1.0, 6.0, ((1, 4),)),
        "counts": plant(jax.random.randint(streams_of[4], (N_GRP * REQ,), 1, SPEC + 1), jax.random.fold_in(streams_of[4], 1), 1, SPEC).astype(jnp.int32),
    }


epsilon = 1e-06

def reference(features, weight, norm_gain, target, counts):
    hidden = jnp.dot(features, weight, preferred_element_type=jnp.float32)
    row_index = jnp.arange(TOKENS, dtype=jnp.int32)
    row_live = (row_index % SPEC < jnp.take(counts, row_index // SPEC)).astype(jnp.float32)[:, None]
    accepted = jnp.sum(counts).astype(jnp.float32)
    squares = lax.optimization_barrier(jnp.sum(hidden * hidden, axis=1, keepdims=True))
    inverse_rms = lax.rsqrt(squares / DOUT + epsilon)
    normed = hidden * inverse_rms * norm_gain[None, :]
    deviation = normed - target.astype(jnp.float32)
    residual = row_live * deviation / accepted
    coupling = lax.optimization_barrier(jnp.sum(norm_gain[None, :] * residual * hidden, axis=1, keepdims=True))
    act_grad = (inverse_rms * norm_gain[None, :] * residual - hidden * inverse_rms ** 3 * coupling / DOUT).astype(jnp.bfloat16)
    weight_grad = lax.dot_general(features, act_grad, (((0,), (0,)), ((), ())), preferred_element_type=jnp.float32).astype(jnp.bfloat16)
    draft_loss = 0.5 * jnp.sum(residual * deviation)
    return (weight_grad, draft_loss)
```

```python
import functools
import jax
import jax.numpy as jnp
from jax import lax
from jax.experimental import pallas as pl
from jax.experimental.pallas import tpu as pltpu
from jax.sharding import PartitionSpec as P

SPEC = 8
epsilon = 1e-06
MIB = 2**20
HBM = pl.BlockSpec(memory_space=pltpu.HBM)
SMEM = pl.BlockSpec(memory_space=pltpu.SMEM)
VMEM = pl.BlockSpec(memory_space=pltpu.VMEM)
bf16, f32 = jnp.bfloat16, jnp.float32


def exchange(value, axis, mask):
    size = lax.axis_size(axis)
    return lax.ppermute(value, axis, [(i, i ^ mask) for i in range(size)])


def after(value, *others):
    return lax.optimization_barrier((value, *others))[0]


def whole(shape):
    return pl.BlockSpec(shape, lambda _: (0,) * len(shape))


def params(mib):
    return pltpu.CompilerParams(vmem_limit_bytes=mib * MIB)


def cost(flops=1024, moved=1024):
    return pl.CostEstimate(flops=flops, bytes_accessed=moved, transcendentals=0)


def copy_kernel(ranges, place_ref, *refs):
    count = len(ranges)
    sources, targets, sems = refs[:count], refs[count : 2 * count], refs[2 * count]
    copies = [
        pltpu.make_async_copy(source.at[pl.ds(start, size), :], target, sems.at[i])
        for i, (source, target, (start, size)) in enumerate(zip(sources, targets, ranges))
    ]
    for copy in copies:
        copy.start()
    for copy in copies:
        copy.wait()


def copy_rows(place, pieces, in_vmem=()):
    shapes = [((size, array.shape[1]), array.dtype) for array, _, size in pieces]
    return pl.pallas_call(
        functools.partial(copy_kernel, [(start, size) for _, start, size in pieces]),
        in_specs=[SMEM] + [HBM] * len(pieces),
        out_specs=[VMEM if i in in_vmem else HBM for i in range(len(pieces))],
        out_shape=[
            pltpu.VMEM(*shape) if i in in_vmem else jax.ShapeDtypeStruct(*shape)
            for i, shape in enumerate(shapes)
        ],
        scratch_shapes=[pltpu.SemaphoreType.DMA((len(pieces),))],
        compiler_params=params(24),
        cost_estimate=cost(),
        name="copy_rows",
    )(place, *[array for array, _, _ in pieces])


def forward_kernel(pieces, tile, place_ref, *refs):
    parts = refs[:pieces]
    weight_ref, keep_out, send_out, rows_ref, keep_ref, send_ref, sems, out_sems = refs[pieces:]
    copies = []
    start = 0
    for i, part in enumerate(parts):
        size = part.shape[0]
        copies.append(pltpu.make_async_copy(part, rows_ref.at[pl.ds(start, size), :], sems.at[i]))
        start += size
    for copy in copies:
        copy.start()
    for copy in copies:
        copy.wait()
    first = place_ref[0] == 0
    turn = place_ref[1]
    slots, half, units = keep_ref.shape
    copies = []
    for step in range(units // tile):
        columns = pl.ds(step * tile, tile)
        product = jnp.dot(
            rows_ref[...], weight_ref[:, columns], preferred_element_type=f32
        )
        for block in range(slots):
            low = product[block * 2 * half : block * 2 * half + half]
            high = product[block * 2 * half + half : (block + 1) * 2 * half]
            slot = block ^ turn
            keep_ref[slot, :, columns] = jnp.where(first, low, high)
            send_ref[slot, :, columns] = jnp.where(first, high, low).astype(bf16)
        for i, (scratch, out) in enumerate(((keep_ref, keep_out), (send_ref, send_out))):
            copies.append(
                pltpu.make_async_copy(
                    scratch.at[:, :, columns], out.at[:, :, columns], out_sems.at[i, step]
                )
            )
            copies[-1].start()
    for copy in copies:
        copy.wait()


def forward(place, parts, weight):
    depth, units = weight.shape
    total_rows = sum(part.shape[0] for part in parts)
    slots = lax.axis_size("grp")
    half = total_rows // slots // 2
    tile = min(units, 512)
    shape = (slots, half, units)
    return pl.pallas_call(
        functools.partial(forward_kernel, len(parts), tile),
        in_specs=[SMEM] + [HBM] * len(parts) + [VMEM],
        out_specs=[HBM, HBM],
        out_shape=[jax.ShapeDtypeStruct(shape, f32), jax.ShapeDtypeStruct(shape, bf16)],
        scratch_shapes=[
            pltpu.VMEM((total_rows, depth), bf16),
            pltpu.VMEM(shape, f32),
            pltpu.VMEM(shape, bf16),
            pltpu.SemaphoreType.DMA((len(parts),)),
            pltpu.SemaphoreType.DMA((2, units // tile)),
        ],
        compiler_params=params(24),
        cost_estimate=cost(),
        name="forward",
    )(place, *parts, weight)


def pair_kernel(place_ref, keep_ref, arrived_ref, own_ref, *sends):
    own_ref[...] = keep_ref[0] + arrived_ref[0].astype(f32)
    for k, send_ref in enumerate(sends, 1):
        send_ref[...] = (keep_ref[k] + arrived_ref[k].astype(f32)).astype(bf16)


def sum_pair(place, keep, arrived):
    slots, half, units = keep.shape
    out = pl.pallas_call(
        pair_kernel,
        grid=(1,),
        in_specs=[SMEM, whole(keep.shape), whole(keep.shape)],
        out_specs=[whole((half, units))] * slots,
        out_shape=[jax.ShapeDtypeStruct((half, units), f32)]
        + [jax.ShapeDtypeStruct((half, units), bf16)] * (slots - 1),
        compiler_params=params(24),
        cost_estimate=cost(),
        name="sum_pair",
    )(place, keep, arrived)
    return out[0], out[1:]


def rows_kernel(place_ref, own_ref, gain_ref, target_ref, *refs):
    arrived, (hidden_ref, sums_ref) = refs[:-2], refs[-2:]
    hidden = own_ref[...]
    for value in arrived:
        hidden = hidden + value[...].astype(f32)
    hidden_ref[...] = hidden
    scaled = hidden * gain_ref[...]
    target = target_ref[...].astype(f32)
    lane = lax.broadcasted_iota(jnp.int32, sums_ref.shape, 1)
    sums = jnp.zeros(sums_ref.shape, f32)
    terms = (hidden * hidden, scaled * scaled, scaled * target, target * target)
    for i, term in enumerate(terms):
        sums = jnp.where(lane == i, jnp.sum(term, axis=1, keepdims=True), sums)
    sums_ref[...] = sums


def sum_planes(place, own, arrived, gain, target):
    half, units = own.shape
    return pl.pallas_call(
        rows_kernel,
        grid=(1,),
        in_specs=[SMEM, whole(own.shape), whole(gain.shape)] + [whole(own.shape)] * (1 + len(arrived)),
        out_specs=[whole(own.shape), whole((half, 128))],
        out_shape=[
            jax.ShapeDtypeStruct((half, units), f32),
            jax.ShapeDtypeStruct((half, 128), f32),
        ],
        compiler_params=params(24),
        cost_estimate=cost(),
        name="sum_planes",
    )(place, own, gain, target, *arrived)


def gradient_kernel(all_units, place_ref, hidden_ref, gain_ref, target_ref, share_ref, *refs):
    all_sums, (grad_ref, loss_ref) = refs[:-2], refs[-2:]
    sums = all_sums[0][...]
    for value in all_sums[1:]:
        sums = sums + value[...]
    squares, scaled_squares = sums[:, 0:1], sums[:, 1:2]
    products, target_squares = sums[:, 2:3], sums[:, 3:4]
    share = share_ref[:, 0:1]
    inverse_rms = lax.rsqrt(squares / all_units + epsilon)
    coupling = share * (inverse_rms * scaled_squares - products)
    loss = inverse_rms * (inverse_rms * scaled_squares - 2.0 * products) + target_squares
    loss_ref[...] = jnp.broadcast_to(
        jnp.sum(0.5 * share * loss, axis=0, keepdims=True), loss_ref.shape
    )
    hidden = hidden_ref[...]
    gain = gain_ref[...]
    residual = share * (hidden * inverse_rms * gain - target_ref[...].astype(f32))
    grad = inverse_rms * gain * residual - hidden * (inverse_rms**3 * coupling / all_units)
    grad_ref[...] = grad.astype(bf16)


def gradient(place, hidden, all_sums, gain, target, share, all_units):
    half, units = hidden.shape
    return pl.pallas_call(
        functools.partial(gradient_kernel, all_units),
        grid=(1,),
        in_specs=[SMEM, whole(hidden.shape), whole(gain.shape), whole(hidden.shape)]
        + [whole((half, 128))] * (1 + len(all_sums)),
        out_specs=[whole(hidden.shape), whole((1, 128))],
        out_shape=[
            jax.ShapeDtypeStruct((half, units), bf16),
            jax.ShapeDtypeStruct((1, 128), f32),
        ],
        compiler_params=params(24),
        cost_estimate=cost(),
        name="gradient",
    )(place, hidden, gain, target, share, *all_sums)


def backward_kernel(piece_counts, slots, has_base, place_ref, *refs):
    count = sum(piece_counts)
    parts, refs = refs[:count], refs[count:]
    grads, refs = refs[: 2 * slots * len(piece_counts)], refs[2 * slots * len(piece_counts) :]
    out_ref, rows_ref = refs[-2:]

    @pl.when(pl.program_id(0) == 0)
    def _():
        core = place_ref[0]
        turn = place_ref[1]
        start = 0
        for chunk in range(len(piece_counts)):
            here = grads[2 * slots * chunk : 2 * slots * (chunk + 1)]
            half = here[0].shape[0]
            for slot in range(slots):
                row = start + (slot ^ turn) * 2 * half
                rows_ref[pl.ds(pl.multiple_of(row + core * half, half), half), :] = here[slot][...]
                rows_ref[pl.ds(pl.multiple_of(row + (1 - core) * half, half), half), :] = here[
                    slots + slot
                ][...]
            start += slots * 2 * half

    left = jnp.concatenate([part[...] for part in parts], axis=0)
    product = lax.dot_general(
        left, rows_ref[...], (((0,), (0,)), ((), ())), preferred_element_type=f32
    )
    if has_base:
        product += refs[0][...].astype(f32)
    out_ref[...] = product.astype(bf16)


def backward(place, chunks, grads, base=None):
    parts = [part for pieces in chunks for part in pieces]
    flat = [grad for pieces in grads for grad in pieces]
    slots = len(grads[0]) // 2
    depth = parts[0].shape[1]
    units = flat[0].shape[1]
    total_rows = sum(part.shape[0] for part in parts)
    tile = min(depth, 512)
    out_spec = pl.BlockSpec((tile, units), lambda k: (k, 0))
    return pl.pallas_call(
        functools.partial(backward_kernel, [len(p) for p in chunks], slots, base is not None),
        grid=(depth // tile,),
        in_specs=[SMEM]
        + [pl.BlockSpec((part.shape[0], tile), lambda k: (0, k)) for part in parts]
        + [pl.BlockSpec(grad.shape, lambda k: (0, 0)) for grad in flat]
        + ([out_spec] if base is not None else []),
        out_specs=out_spec,
        out_shape=jax.ShapeDtypeStruct((depth, units), bf16),
        scratch_shapes=[pltpu.VMEM((total_rows, units), bf16)],
        compiler_params=params(34),
        cost_estimate=cost(2 * total_rows * depth * units, 4 * depth * units),
        name="backward",
    )(place, *parts, *flat, *([] if base is None else [base]))


def piece_rows(rows):
    return [rows // 4] * 4


def shards(features, weight, norm_gain, target, counts):
    groups = lax.axis_size("grp")
    group, place_tp = lax.axis_index("grp"), lax.axis_index("tp")
    core, plane = place_tp % 2, place_tp // 2
    place = jnp.stack([core, plane ^ group]).astype(jnp.int32)
    group_rows = features.shape[0]
    all_units = norm_gain.shape[0] * groups
    gain = norm_gain[None, :]

    sizes = piece_rows(group_rows)
    n = len(sizes)
    starts = [sum(sizes[:i]) for i in range(n)]

    accepted = jnp.sum(counts).astype(f32)
    requests = group_rows // SPEC
    here = lax.dynamic_slice_in_dim(counts, plane * requests, requests, 0)
    live = (jnp.arange(SPEC, dtype=jnp.int32)[None, :] < here[:, None]).astype(f32) / accepted
    live = jnp.broadcast_to(live.reshape(group_rows, 1), (group_rows, 128))
    shares, targets = [], []
    for start, size in zip(starts, sizes):
        row, half = start + core * (size // 2), size // 2
        shares.append(lax.dynamic_slice_in_dim(live, row, half, 0))
        targets.append(lax.dynamic_slice_in_dim(target, plane * group_rows + row, half, 0))

    last = [place]

    def turn(*waits):
        return after(place, *last, *waits)

    def ran(outputs):
        last[:] = jax.tree.leaves(outputs)
        return outputs

    own, edge, corner = ([None] * n for _ in range(3))
    keep, send, mine, sends, hidden, sums, grads = ([None] * n for _ in range(7))
    losses = [None] * n

    def send_own(i):
        if groups == 4:
            edge[i] = [exchange(own[i], "grp", 1), exchange(own[i], "grp", 2)]
            return
        blocks = [own[i]]
        mask = 1
        while mask < groups:
            blocks += [exchange(block, "grp", mask) for block in blocks]
            mask *= 2
        edge[i], corner[i] = blocks[1:], []

    def send_corner(i, *copied):
        pieces = [(features, starts[j], sizes[j]) for j in copied]
        if groups == 4:
            half = sizes[i] // 2
            pieces = [(edge[i][0], 0, half), (edge[i][1], half, half)] + pieces
        if not pieces:
            return
        out = ran(copy_rows(turn(*edge[i]), pieces))
        if groups == 4:
            corner[i] = [exchange(out[0], "grp", 2), exchange(out[1], "grp", 1)]
            out = out[2:]
        for j, value in zip(copied, out):
            own[j] = value
            send_own(j)

    def multiply(i, *waits):
        parts = [own[i], *edge[i], *corner[i]]
        keep[i], send[i] = ran(forward(turn(*parts, *waits), parts, weight_here))

    def add_pair(i):
        arrived = exchange(send[i], "tp", 1)
        mine[i], out = ran(sum_pair(turn(arrived), keep[i], arrived))
        sends[i] = [exchange(value, "tp", 2 * k) for k, value in enumerate(out, 1)]

    def add_planes(i):
        hidden[i], part = ran(
            sum_planes(turn(*sends[i]), mine[i], sends[i], gain, targets[i])
        )
        sums[i] = [part] + [exchange(part, "grp", mask) for mask in range(1, groups)]

    def differentiate(i):
        grad, losses[i] = ran(
            gradient(turn(*sums[i]), hidden[i], sums[i], gain, targets[i], shares[i], all_units)
        )
        slots = [grad] + [exchange(grad, "tp", 2 * k) for k in range(1, groups)]
        grads[i] = slots + [exchange(value, "tp", 1) for value in slots]

    own[0], own[1] = ran(copy_rows(turn(), [(features, starts[j], sizes[j]) for j in (0, 1)]))
    send_own(0)
    send_own(1)
    ran([*targets, *shares])
    send_corner(0, 2)
    send_corner(1, 3)
    (weight_here,) = copy_rows(turn(), [(weight, 0, weight.shape[0])], in_vmem=(0,))
    weight_here = pltpu.with_memory_space_constraint(weight_here, pltpu.VMEM)
    multiply(0)
    add_pair(0)
    send_corner(2)
    multiply(1)
    add_pair(1)
    add_planes(0)
    send_corner(3)
    differentiate(0)
    multiply(2)
    add_pair(2)
    add_planes(1)
    multiply(3)
    add_pair(3)
    differentiate(1)
    add_planes(2)
    add_planes(3)
    differentiate(2)
    differentiate(3)
    chunks = [[own[i], *edge[i], *corner[i]] for i in range(n)]
    loss = sum(losses)
    loss = loss + exchange(loss, "tp", 1)
    loss_parts = [loss] + [exchange(loss, "tp", 2 * k) for k in range(1, groups)]
    waits = [value for pieces in grads for value in pieces]
    weight_grad = backward(turn(loss, *waits), chunks, grads)
    draft_loss = sum(loss_parts)[0, 0]
    return (weight_grad, draft_loss)


def solution(mesh):
    placed = (P("grp", "tp"), P("tp", "grp"), P("grp"), P(None, "grp"), P())
    return jax.shard_map(
        shards, mesh=mesh, in_specs=placed, out_specs=(P("tp", "grp"), P()), check_vma=False
    )
```

```python
import functools
import jax
import jax.numpy as jnp
from jax import lax
from jax.experimental import pallas as pl
from jax.experimental.pallas import tpu as pltpu
from jax.sharding import PartitionSpec as P

SPEC = 8
epsilon = 1e-06
MIB = 2**20
ROWS = 16
PARTS = 2
HBM = pl.BlockSpec(memory_space=pltpu.HBM)
SMEM = pl.BlockSpec(memory_space=pltpu.SMEM)
VMEM = pl.BlockSpec(memory_space=pltpu.VMEM)
bf16, f32 = jnp.bfloat16, jnp.float32


def exchange(value, axis, mask):
    size = lax.axis_size(axis)
    return lax.ppermute(value, axis, [(i, i ^ mask) for i in range(size)])


def in_hbm(*arrays):
    return [pltpu.with_memory_space_constraint(array, pltpu.HBM) for array in arrays]


def after(value, *others):
    return lax.optimization_barrier((value, *others))[0]


def whole(shape):
    return pl.BlockSpec(shape, lambda _: (0,) * len(shape))


def params(mib):
    return pltpu.CompilerParams(vmem_limit_bytes=mib * MIB)


def cost(flops=1024, moved=1024):
    return pl.CostEstimate(flops=flops, bytes_accessed=moved, transcendentals=0)


def run_copies(copies):
    for copy in copies:
        copy.start()
    for copy in copies:
        copy.wait()


def copy_kernel(ranges, place_ref, *refs):
    count = len(ranges)
    sources, targets, holds, sems = refs[:count], refs[count : 2 * count], refs[2 * count : -1], refs[-1]
    into = [
        pltpu.make_async_copy(source.at[pl.ds(start, size), :], hold, sems.at[0, i])
        for i, (source, hold, (start, size)) in enumerate(zip(sources, holds, ranges))
    ]
    out = [
        pltpu.make_async_copy(hold, target, sems.at[1, i])
        for i, (hold, target) in enumerate(zip(holds, targets))
    ]
    for copy in into:
        copy.start()
    for first, second in zip(into, out):
        first.wait()
        second.start()
    for copy in out:
        copy.wait()


def copy_rows(place, pieces):
    shapes = [((size, array.shape[1]), array.dtype) for array, _, size in pieces]
    return pl.pallas_call(
        functools.partial(copy_kernel, [(start, size) for _, start, size in pieces]),
        in_specs=[SMEM] + [HBM] * len(pieces),
        out_specs=[HBM] * len(pieces),
        out_shape=[pltpu.HBM(*shape) for shape in shapes],
        scratch_shapes=[pltpu.VMEM(*shape) for shape in shapes]
        + [pltpu.SemaphoreType.DMA((2, len(pieces)))],
        compiler_params=params(12),
        cost_estimate=cost(),
        name="copy_rows",
    )(place, *in_hbm(*[array for array, _, _ in pieces]))


def load_kernel(place_ref, source_ref, target_ref, sem):
    run_copies([pltpu.make_async_copy(source_ref, target_ref, sem)])


def load(place, array):
    held = pl.pallas_call(
        load_kernel,
        in_specs=[SMEM, HBM],
        out_specs=VMEM,
        out_shape=pltpu.VMEM(array.shape, array.dtype),
        scratch_shapes=[pltpu.SemaphoreType.DMA],
        compiler_params=params(12),
        cost_estimate=cost(),
        name="load",
    )(place, *in_hbm(array))
    return pltpu.with_memory_space_constraint(held, pltpu.VMEM)


def forward_kernel(pieces, tile, place_ref, *refs):
    parts = refs[:pieces]
    weight_ref, keep_out, send_out, rows_ref, keep_ref, send_ref, sems, out_sems = refs[pieces:]
    copies = []
    start = 0
    for i, part in enumerate(parts):
        size = part.shape[0]
        copies.append(pltpu.make_async_copy(part, rows_ref.at[pl.ds(start, size), :], sems.at[i]))
        start += size
    run_copies(copies)
    shape = keep_ref.shape[:-1]
    units = keep_ref.shape[-1]
    for column in range(0, units, tile):
        columns = slice(column, column + tile)
        product = jnp.dot(
            rows_ref[...], weight_ref[:, columns], preferred_element_type=f32
        ).reshape(*shape, tile)
        keep_ref[..., columns] = product
        send_ref[..., columns] = product.astype(bf16)
    core, plane = place_ref[0], place_ref[1]
    copies = []
    for slot in range(keep_out.shape[0]):
        owner = (plane ^ slot) * 2
        copies += [
            pltpu.make_async_copy(
                keep_ref.at[:, owner + core], keep_out.at[slot], out_sems.at[0, slot]
            ),
            pltpu.make_async_copy(
                send_ref.at[:, owner + 1 - core], send_out.at[slot], out_sems.at[1, slot]
            ),
        ]
    run_copies(copies)


def forward(place, blocks, weight, slots):
    depth, units = weight.shape
    parts = [part for block in blocks for part in block]
    total_rows = sum(part.shape[0] for part in parts)
    count = len(blocks)
    tile = min(units, 512)
    scratch = (count, 2 * slots, ROWS, units)
    shape = (slots, count, ROWS, units)
    keep, send = pl.pallas_call(
        functools.partial(forward_kernel, len(parts), tile),
        in_specs=[SMEM] + [HBM] * len(parts) + [VMEM],
        out_specs=[HBM, HBM],
        out_shape=[pltpu.HBM(shape, f32), pltpu.HBM(shape, bf16)],
        scratch_shapes=[
            pltpu.VMEM((total_rows, depth), bf16),
            pltpu.VMEM(scratch, f32),
            pltpu.VMEM(scratch, bf16),
            pltpu.SemaphoreType.DMA((len(parts),)),
            pltpu.SemaphoreType.DMA((2, slots)),
        ],
        compiler_params=params(12),
        cost_estimate=cost(),
        name="forward",
    )(place, *in_hbm(*parts), weight)
    shape = (slots, count * ROWS, units)
    return keep.reshape(shape), send.reshape(shape)


def pair_kernel(count, place_ref, *refs):
    keeps, arrived = refs[:count], refs[count : 2 * count]
    own_ref, *sends = refs[2 * count :]
    start = 0
    for keep_ref, arrived_ref in zip(keeps, arrived):
        rows = pl.ds(start, keep_ref.shape[1])
        own_ref[rows, :] = keep_ref[0] + arrived_ref[0].astype(f32)
        for k, send_ref in enumerate(sends, 1):
            send_ref[rows, :] = (keep_ref[k] + arrived_ref[k].astype(f32)).astype(bf16)
        start += keep_ref.shape[1]


def sum_pair(place, events):
    keeps, arrived = zip(*events)
    slots, _, units = keeps[0].shape
    rows = sum(keep.shape[1] for keep in keeps)
    out = pl.pallas_call(
        functools.partial(pair_kernel, len(keeps)),
        grid=(1,),
        in_specs=[SMEM] + [whole(keep.shape) for keep in keeps] * 2,
        out_specs=[whole((rows, units))] * slots,
        out_shape=[jax.ShapeDtypeStruct((rows, units), f32)]
        + [jax.ShapeDtypeStruct((rows, units), bf16)] * (slots - 1),
        compiler_params=params(12),
        cost_estimate=cost(),
        name="sum_pair",
    )(place, *keeps, *arrived)
    return out[0], out[1:]


def planes_kernel(place_ref, own_ref, *refs):
    arrived, hidden_ref = refs[:-1], refs[-1]
    hidden = own_ref[...]
    for value in arrived:
        hidden = hidden + value[...].astype(f32)
    hidden_ref[...] = hidden


def sum_planes(place, own, arrived):
    return pl.pallas_call(
        planes_kernel,
        grid=(1,),
        in_specs=[SMEM] + [whole(own.shape)] * (1 + len(arrived)),
        out_specs=whole(own.shape),
        out_shape=jax.ShapeDtypeStruct(own.shape, f32),
        compiler_params=params(12),
        cost_estimate=cost(),
        name="sum_planes",
    )(place, own, *arrived)


def targets_kernel(group_rows, sets, groups, place_ref, target_ref, out_ref, hold_ref, sems):
    core, plane, group = place_ref[0], place_ref[1], place_ref[2]
    span = group_rows // sets
    copies = []
    for i in range(sets):
        for block in range(groups):
            row = (group ^ block) * group_rows + i * span + (plane * 2 + core) * ROWS
            copies.append(
                pltpu.make_async_copy(
                    target_ref.at[pl.ds(pl.multiple_of(row, ROWS), ROWS), :],
                    hold_ref.at[pl.ds((i * groups + block) * ROWS, ROWS), :],
                    sems.at[i * groups + block],
                )
            )
    run_copies(copies)
    run_copies([pltpu.make_async_copy(hold_ref, out_ref, sems.at[sets * groups])])


def take_targets(place, target, group_rows, sets, groups):
    shape = (sets * groups * ROWS, target.shape[1])
    return pl.pallas_call(
        functools.partial(targets_kernel, group_rows, sets, groups),
        in_specs=[SMEM, HBM],
        out_specs=HBM,
        out_shape=pltpu.HBM(shape, bf16),
        scratch_shapes=[
            pltpu.VMEM(shape, bf16),
            pltpu.SemaphoreType.DMA((sets * groups + 1,)),
        ],
        compiler_params=params(12),
        cost_estimate=cost(),
        name="take_targets",
    )(place, *in_hbm(target))


def rows_kernel(ranges, late, place_ref, gain_ref, target_ref, *refs):
    early, (own_ref, *arrived), (hidden_ref, sums_ref) = (
        refs[: len(ranges)],
        refs[len(ranges) : len(ranges) + 1 + late],
        refs[-2:],
    )
    last = own_ref[...]
    for value in arrived:
        last = last + value[...].astype(f32)
    parts = [ref[start : start + size, :] for ref, (start, size) in zip(early, ranges)]
    hidden = jnp.concatenate(parts + [last], axis=0)
    hidden_ref[...] = hidden
    scaled = hidden * gain_ref[...]
    target = target_ref[...].astype(f32)
    lane = lax.broadcasted_iota(jnp.int32, sums_ref.shape, 1)
    sums = jnp.zeros(sums_ref.shape, f32)
    terms = (hidden * hidden, scaled * scaled, scaled * target, target * target)
    for i, term in enumerate(terms):
        sums = jnp.where(lane == i, jnp.sum(term, axis=1, keepdims=True), sums)
    sums_ref[...] = sums


def sum_rows(place, early, own, arrived, gain, target):
    rows, units = target.shape
    return pl.pallas_call(
        functools.partial(rows_kernel, [(b, c) for _, b, c in early], len(arrived)),
        grid=(1,),
        in_specs=[SMEM, whole(gain.shape), whole(target.shape)]
        + [whole(array.shape) for array, _, _ in early]
        + [whole(own.shape)] * (1 + len(arrived)),
        out_specs=[whole((rows, units)), whole((rows, 128))],
        out_shape=[
            jax.ShapeDtypeStruct((rows, units), f32),
            jax.ShapeDtypeStruct((rows, 128), f32),
        ],
        compiler_params=params(12),
        cost_estimate=cost(),
        name="sum_rows",
    )(place, gain, target, *[array for array, _, _ in early], own, *arrived)


def gradient_kernel(all_units, place_ref, hidden_ref, gain_ref, target_ref, share_ref, *refs):
    all_sums, grads = refs[:-PARTS], refs[-PARTS:]
    rows = hidden_ref.shape[0]
    sums = jnp.concatenate(
        [
            sum(ref[(block ^ k) * ROWS : ((block ^ k) + 1) * ROWS, :] for k, ref in enumerate(all_sums))
            for block in range(rows // ROWS)
        ],
        axis=0,
    )
    squares, scaled_squares = sums[:, 0:1], sums[:, 1:2]
    products, target_squares = sums[:, 2:3], sums[:, 3:4]
    share = share_ref[:, 0:1]
    inverse_rms = lax.rsqrt(squares / all_units + epsilon)
    coupling = share * (inverse_rms * scaled_squares - products)
    loss = inverse_rms * (inverse_rms * scaled_squares - 2.0 * products) + target_squares
    loss = jnp.broadcast_to(jnp.sum(0.5 * share * loss, axis=0, keepdims=True), (loss.shape[0], 128))
    first = loss.astype(bf16)
    second = (loss - first.astype(f32)).astype(bf16)
    third = (loss - first.astype(f32) - second.astype(f32)).astype(bf16)
    lane = lax.broadcasted_iota(jnp.int32, loss.shape, 1)
    third = jnp.where(lane == 2, third.astype(f32), 0.0)
    loss = jnp.where(lane == 1, second.astype(f32), third)
    loss = jnp.where(lane == 0, first.astype(f32), loss).astype(bf16)
    hidden = hidden_ref[...]
    gain = gain_ref[...]
    residual = share * (hidden * inverse_rms * gain - target_ref[...].astype(f32))
    grad = inverse_rms * gain * residual - hidden * (inverse_rms**3 * coupling / all_units)
    width = hidden.shape[1] // PARTS
    for i, grad_ref in enumerate(grads):
        grad_ref[:, :width] = grad[:, i * width : (i + 1) * width].astype(bf16)
        if i == 0:
            grad_ref[:, width:] = loss


def gradient(place, hidden, all_sums, gain, target, share, all_units):
    rows, units = hidden.shape
    shapes = [(rows, units // PARTS + (128 if i == 0 else 0)) for i in range(PARTS)]
    return pl.pallas_call(
        functools.partial(gradient_kernel, all_units),
        grid=(1,),
        in_specs=[SMEM, whole(hidden.shape), whole(gain.shape), whole(hidden.shape)]
        + [whole((rows, 128))] * (1 + len(all_sums)),
        out_specs=[whole(shape) for shape in shapes],
        out_shape=[jax.ShapeDtypeStruct(shape, bf16) for shape in shapes],
        compiler_params=params(12),
        cost_estimate=cost(),
        name="gradient",
    )(place, hidden, gain, target, share, *all_sums)


def piece_copies(place_ref, pieces, target, sems):
    core, plane = place_ref[0], place_ref[1]
    slots = len(pieces) // 2
    copies = []
    for i, piece in enumerate(pieces):
        owner = (plane ^ (i % slots)) * 2 + (core if i < slots else 1 - core)
        copies.append(
            pltpu.make_async_copy(piece, target.at[:, owner], sems.at[i])
        )
    return copies


def by_block(pieces):
    return in_hbm(*[piece.reshape(piece.shape[0] // ROWS, ROWS, -1) for piece in pieces])


def backward_kernel(part_count, piece_count, place_ref, *refs):
    parts, refs = refs[:part_count], refs[part_count:]
    pieces, refs = refs[:piece_count], refs[piece_count:]
    rows_ref, sems = refs[-2:]
    out_ref, *loss = refs[-4:-2] if refs[-3].shape[-1] == 128 else refs[-3:-2]
    units = out_ref.shape[-1]

    @pl.when(pl.program_id(0) == 0)
    def _():
        run_copies(piece_copies(place_ref, pieces, rows_ref, sems))
        for loss_ref in loss:
            total = jnp.zeros(loss_ref.shape, f32)
            for owner in range(rows_ref.shape[1]):
                total += rows_ref[0, owner, :, units:].astype(f32)
            loss_ref[...] = total

    left = jnp.concatenate([part[...] for part in parts], axis=0)
    out_ref[...] = lax.dot_general(
        left,
        rows_ref[..., :units].reshape(left.shape[0], units),
        (((0,), (0,)), ((), ())),
        preferred_element_type=f32,
    ).astype(bf16)


def backward(place, parts, pieces, index, units, result=None):
    depth = parts[0].shape[1]
    tile = min(depth, 1024)
    width = units // PARTS
    blocks = pieces[0].shape[0] // ROWS
    operands = [place, *in_hbm(*parts), *by_block(pieces)]
    first = result is None
    out = pl.pallas_call(
        functools.partial(backward_kernel, len(parts), len(pieces)),
        grid=(depth // tile,),
        in_specs=[SMEM]
        + [pl.BlockSpec((part.shape[0], tile), lambda k: (0, k)) for part in parts]
        + [HBM] * (len(pieces) + (not first)),
        out_specs=[pl.BlockSpec((tile, width), lambda k: (k, index))]
        + [pl.BlockSpec((ROWS, 128), lambda k: (0, 0))] * first,
        out_shape=[jax.ShapeDtypeStruct((depth, units), bf16)]
        + [jax.ShapeDtypeStruct((ROWS, 128), f32)] * first,
        scratch_shapes=[
            pltpu.VMEM((blocks, len(pieces), ROWS, pieces[0].shape[1]), bf16),
            pltpu.SemaphoreType.DMA((len(pieces),)),
        ],
        input_output_aliases={} if first else {len(operands): 0},
        compiler_params=params(24),
        cost_estimate=cost(),
        name="backward",
    )(*operands, *([] if first else [result]))
    return out if first else [out[0], None]


def shards(features, weight, norm_gain, target, counts):
    groups, tp = lax.axis_size("grp"), lax.axis_size("tp")
    group, place_tp = lax.axis_index("grp"), lax.axis_index("tp")
    core, plane = place_tp % 2, place_tp // 2
    slots = tp // 2
    place = jnp.stack([core, plane, group]).astype(jnp.int32)
    group_rows = features.shape[0]
    all_units = norm_gain.shape[0] * groups
    gain = norm_gain[None, :]
    span = ROWS * tp
    sets = range(group_rows // span)

    accepted = jnp.sum(counts).astype(f32)
    blocks = group ^ jnp.arange(groups, dtype=jnp.int32)
    index = (
        jnp.arange(len(sets), dtype=jnp.int32)[:, None, None] * span
        + blocks[None, :, None] * group_rows
        + (plane * 2 + core) * ROWS
        + jnp.arange(ROWS, dtype=jnp.int32)[None, None, :]
    ).reshape(len(sets), groups * ROWS)
    live = (index % SPEC < jnp.take(counts, index // SPEC)).astype(f32) / accepted
    share = jnp.broadcast_to(live.reshape(-1, 1), (live.size, 128))

    last = [place]

    def turn(*waits):
        return after(place, *last, *waits)

    def ran(outputs):
        last[:] = jax.tree.leaves(outputs)
        return outputs

    own = ran(copy_rows(turn(), [(features, i * span, span) for i in sets]))
    block_rows = [{0: [own[i]]} for i in sets]
    for i in sets:
        if groups == 4:
            block_rows[i][1] = [exchange(own[i], "grp", 1)]
            block_rows[i][2] = [exchange(own[i], "grp", 2)]
        else:
            mask = 1
            while mask < groups:
                for block in range(mask):
                    block_rows[i][block ^ mask] = [exchange(block_rows[i][block][0], "grp", mask)]
                mask *= 2

    def send_corner(i):
        (first,), (second,) = block_rows[i][1], block_rows[i][2]
        half = span // 2
        low, high = ran(copy_rows(turn(first, second), [(first, 0, half), (second, half, half)]))
        block_rows[i][3] = [exchange(low, "grp", 2), exchange(high, "grp", 1)]

    def multiply(pieces):
        rows = [block_rows[i][block] for i, block in pieces]
        keep, send = ran(
            forward(turn(*[part for parts in rows for part in parts]), rows, weight_here, slots)
        )
        return keep, exchange(send, "tp", 1)

    def add_pair(*events):
        own_sum, out = ran(sum_pair(turn(*[arrived for _, arrived in events]), events))
        return own_sum, [exchange(value, "tp", 2 * k) for k, value in enumerate(out, 1)]

    def add_planes(own_sum, arrived):
        return ran(sum_planes(turn(*arrived), own_sum, arrived))

    def add_rows(early, own_sum, arrived):
        hidden, part = ran(sum_rows(turn(*arrived), early, own_sum, arrived, gain, targets))
        return hidden, [part] + [exchange(part, "grp", mask) for mask in range(1, groups)]

    def differentiate(hidden, sums):
        return ran(gradient(turn(*sums), hidden, sums, gain, targets, share, all_units))

    def spread(grad, *waits):
        grad = after(grad, *waits)
        return [grad] + [exchange(grad, "tp", 2 * k) for k in range(1, slots)]

    def spread_pair(pieces, *waits):
        return pieces + [exchange(after(value, *waits), "tp", 1) for value in pieces]

    weight_here = load(turn(), weight)
    targets = ran(take_targets(turn(share), target, group_rows, len(sets), groups))
    own_pair = multiply([(i, 0) for i in sets])
    own_planes = add_pair(own_pair)
    if groups == 4 and len(sets) == 2:
        send_corner(0)
        edge0 = multiply([(0, 1), (0, 2)])
        own_hidden = add_planes(*own_planes)
        edge0 = add_pair(edge0)
        send_corner(1)
        edge1 = multiply([(1, 1), (1, 2)])
        hidden0 = add_planes(*edge0)
        corner0 = multiply([(0, 3)])
        late1 = add_pair(edge1, corner0)
        corner1 = add_pair(multiply([(1, 3)]))
        hidden1 = add_planes(*late1)
        early = [
            (own_hidden, 0, ROWS),
            (hidden0, 0, 2 * ROWS),
            (hidden1, 2 * ROWS, ROWS),
            (own_hidden, ROWS, ROWS),
            (hidden1, 0, 2 * ROWS),
        ]
        rows = add_rows(early, *corner1)
    else:
        own_hidden = add_planes(*own_planes)
        early = []
        for i in sets:
            early.append((own_hidden, i * ROWS, ROWS))
            for block in range(1, groups):
                pair = add_pair(multiply([(i, block)]))
                if (i, block) != (sets[-1], groups - 1):
                    early.append((add_planes(*pair), 0, ROWS))
        rows = add_rows(early, *pair)
    grads = differentiate(*rows)
    parts = [part for i in sets for block in range(groups) for part in block_rows[i][block]]
    planes = []
    for grad in grads:
        planes.append(spread(grad, *[pieces[1] for pieces in planes[-1:]]))
    result = loss = None
    for i, pieces in enumerate(planes):
        pieces = spread_pair(pieces, *([] if i == 0 else [loss]))
        result, total = backward(turn(*pieces), parts, pieces, i, gain.shape[1], result)
        loss = total if i == 0 else loss
        ran(loss)
    return (result, jnp.sum(loss[0]))


def solution(mesh):
    placed = (P("grp", "tp"), P("tp", "grp"), P("grp"), P(None, "grp"), P())
    return jax.shard_map(
        shards, mesh=mesh, in_specs=placed, out_specs=(P("tp", "grp"), P()), check_vma=False
    )
```

```python
import functools
import jax
import jax.numpy as jnp
from jax import lax
from jax.experimental import pallas as pl
from jax.experimental.pallas import tpu as pltpu
from jax.sharding import PartitionSpec as P

SPEC = 8
epsilon = 1e-06
MIB = 2**20
ROWS = 16
PARTS = 2
HBM = pl.BlockSpec(memory_space=pltpu.HBM)
SMEM = pl.BlockSpec(memory_space=pltpu.SMEM)
VMEM = pl.BlockSpec(memory_space=pltpu.VMEM)
bf16, f32 = jnp.bfloat16, jnp.float32


def exchange(value, axis, mask):
    size = lax.axis_size(axis)
    return lax.ppermute(value, axis, [(i, i ^ mask) for i in range(size)])


def in_hbm(*arrays):
    return [pltpu.with_memory_space_constraint(array, pltpu.HBM) for array in arrays]


def after(value, *others):
    return lax.optimization_barrier((value, *others))[0]


def whole(shape):
    return pl.BlockSpec(shape, lambda _: (0,) * len(shape))


def params(mib):
    return pltpu.CompilerParams(vmem_limit_bytes=mib * MIB)


def cost(flops=1024, moved=1024):
    return pl.CostEstimate(flops=flops, bytes_accessed=moved, transcendentals=0)


def run_copies(copies):
    for copy in copies:
        copy.start()
    for copy in copies:
        copy.wait()


def copy_kernel(ranges, place_ref, *refs):
    count = len(ranges)
    sources, targets, holds, sems = refs[:count], refs[count : 2 * count], refs[2 * count : -1], refs[-1]
    into = [
        pltpu.make_async_copy(source.at[pl.ds(start, size), :], hold, sems.at[0, i])
        for i, (source, hold, (start, size)) in enumerate(zip(sources, holds, ranges))
    ]
    out = [
        pltpu.make_async_copy(hold, target, sems.at[1, i])
        for i, (hold, target) in enumerate(zip(holds, targets))
    ]
    for copy in into:
        copy.start()
    for first, second in zip(into, out):
        first.wait()
        second.start()
    for copy in out:
        copy.wait()


def copy_rows(place, pieces):
    shapes = [((size, array.shape[1]), array.dtype) for array, _, size in pieces]
    return pl.pallas_call(
        functools.partial(copy_kernel, [(start, size) for _, start, size in pieces]),
        in_specs=[SMEM] + [HBM] * len(pieces),
        out_specs=[HBM] * len(pieces),
        out_shape=[pltpu.HBM(*shape) for shape in shapes],
        scratch_shapes=[pltpu.VMEM(*shape) for shape in shapes]
        + [pltpu.SemaphoreType.DMA((2, len(pieces)))],
        compiler_params=params(12),
        cost_estimate=cost(),
        name="copy_rows",
    )(place, *in_hbm(*[array for array, _, _ in pieces]))


def load_kernel(place_ref, source_ref, target_ref, sem):
    run_copies([pltpu.make_async_copy(source_ref, target_ref, sem)])


def load(place, array):
    held = pl.pallas_call(
        load_kernel,
        in_specs=[SMEM, HBM],
        out_specs=VMEM,
        out_shape=pltpu.VMEM(array.shape, array.dtype),
        scratch_shapes=[pltpu.SemaphoreType.DMA],
        compiler_params=params(12),
        cost_estimate=cost(),
        name="load",
    )(place, *in_hbm(array))
    return pltpu.with_memory_space_constraint(held, pltpu.VMEM)


def forward_kernel(pieces, tile, place_ref, *refs):
    parts = refs[:pieces]
    weight_ref, keep_out, send_out, rows_ref, keep_ref, send_ref, sems, out_sems = refs[pieces:]
    copies = []
    start = 0
    for i, part in enumerate(parts):
        size = part.shape[0]
        copies.append(pltpu.make_async_copy(part, rows_ref.at[pl.ds(start, size), :], sems.at[i]))
        start += size
    run_copies(copies)
    shape = keep_ref.shape[:-1]
    units = keep_ref.shape[-1]
    for column in range(0, units, tile):
        columns = slice(column, column + tile)
        product = jnp.dot(
            rows_ref[...], weight_ref[:, columns], preferred_element_type=f32
        ).reshape(*shape, tile)
        keep_ref[..., columns] = product
        send_ref[..., columns] = product.astype(bf16)
    core, plane = place_ref[0], place_ref[1]
    copies = []
    for slot in range(keep_out.shape[0]):
        owner = (plane ^ slot) * 2
        copies += [
            pltpu.make_async_copy(
                keep_ref.at[:, owner + core], keep_out.at[slot], out_sems.at[0, slot]
            ),
            pltpu.make_async_copy(
                send_ref.at[:, owner + 1 - core], send_out.at[slot], out_sems.at[1, slot]
            ),
        ]
    run_copies(copies)


def forward(place, blocks, weight, slots):
    depth, units = weight.shape
    parts = [part for block in blocks for part in block]
    total_rows = sum(part.shape[0] for part in parts)
    count = len(blocks)
    tile = min(units, 512)
    scratch = (count, 2 * slots, ROWS, units)
    shape = (slots, count, ROWS, units)
    keep, send = pl.pallas_call(
        functools.partial(forward_kernel, len(parts), tile),
        in_specs=[SMEM] + [HBM] * len(parts) + [VMEM],
        out_specs=[HBM, HBM],
        out_shape=[pltpu.HBM(shape, f32), pltpu.HBM(shape, bf16)],
        scratch_shapes=[
            pltpu.VMEM((total_rows, depth), bf16),
            pltpu.VMEM(scratch, f32),
            pltpu.VMEM(scratch, bf16),
            pltpu.SemaphoreType.DMA((len(parts),)),
            pltpu.SemaphoreType.DMA((2, slots)),
        ],
        compiler_params=params(12),
        cost_estimate=cost(),
        name="forward",
    )(place, *in_hbm(*parts), weight)
    shape = (slots, count * ROWS, units)
    return keep.reshape(shape), send.reshape(shape)


def pair_kernel(count, place_ref, *refs):
    keeps, arrived = refs[:count], refs[count : 2 * count]
    own_ref, *sends = refs[2 * count :]
    start = 0
    for keep_ref, arrived_ref in zip(keeps, arrived):
        rows = pl.ds(start, keep_ref.shape[1])
        own_ref[rows, :] = keep_ref[0] + arrived_ref[0].astype(f32)
        for k, send_ref in enumerate(sends, 1):
            send_ref[rows, :] = (keep_ref[k] + arrived_ref[k].astype(f32)).astype(bf16)
        start += keep_ref.shape[1]


def sum_pair(place, events):
    keeps, arrived = zip(*events)
    slots, _, units = keeps[0].shape
    rows = sum(keep.shape[1] for keep in keeps)
    out = pl.pallas_call(
        functools.partial(pair_kernel, len(keeps)),
        grid=(1,),
        in_specs=[SMEM] + [whole(keep.shape) for keep in keeps] * 2,
        out_specs=[whole((rows, units))] * slots,
        out_shape=[jax.ShapeDtypeStruct((rows, units), f32)]
        + [jax.ShapeDtypeStruct((rows, units), bf16)] * (slots - 1),
        compiler_params=params(12),
        cost_estimate=cost(),
        name="sum_pair",
    )(place, *keeps, *arrived)
    return out[0], out[1:]


def planes_kernel(place_ref, own_ref, *refs):
    arrived, hidden_ref = refs[:-1], refs[-1]
    hidden = own_ref[...]
    for value in arrived:
        hidden = hidden + value[...].astype(f32)
    hidden_ref[...] = hidden


def sum_planes(place, own, arrived):
    return pl.pallas_call(
        planes_kernel,
        grid=(1,),
        in_specs=[SMEM] + [whole(own.shape)] * (1 + len(arrived)),
        out_specs=whole(own.shape),
        out_shape=jax.ShapeDtypeStruct(own.shape, f32),
        compiler_params=params(12),
        cost_estimate=cost(),
        name="sum_planes",
    )(place, own, *arrived)


def targets_kernel(group_rows, sets, groups, place_ref, target_ref, out_ref, hold_ref, sems):
    core, plane, group = place_ref[0], place_ref[1], place_ref[2]
    span = group_rows // sets
    copies = []
    for i in range(sets):
        for block in range(groups):
            row = (group ^ block) * group_rows + i * span + (plane * 2 + core) * ROWS
            copies.append(
                pltpu.make_async_copy(
                    target_ref.at[pl.ds(pl.multiple_of(row, ROWS), ROWS), :],
                    hold_ref.at[pl.ds((i * groups + block) * ROWS, ROWS), :],
                    sems.at[i * groups + block],
                )
            )
    run_copies(copies)
    run_copies([pltpu.make_async_copy(hold_ref, out_ref, sems.at[sets * groups])])


def take_targets(place, target, group_rows, sets, groups):
    shape = (sets * groups * ROWS, target.shape[1])
    return pl.pallas_call(
        functools.partial(targets_kernel, group_rows, sets, groups),
        in_specs=[SMEM, HBM],
        out_specs=HBM,
        out_shape=pltpu.HBM(shape, bf16),
        scratch_shapes=[
            pltpu.VMEM(shape, bf16),
            pltpu.SemaphoreType.DMA((sets * groups + 1,)),
        ],
        compiler_params=params(12),
        cost_estimate=cost(),
        name="take_targets",
    )(place, *in_hbm(target))


def rows_kernel(ranges, late, place_ref, gain_ref, target_ref, *refs):
    own_ref, *arrived = refs[: 1 + late]
    early, (hidden_ref, sums_ref) = list(refs[1 + late : -2]), refs[-2:]
    last = own_ref[...]
    for value in arrived:
        last = last + value[...].astype(f32)
    parts = []
    for is_early, start, size in ranges:
        part = early.pop(0)[...] if is_early else last
        parts.append(part[start : start + size, :])
    hidden = jnp.concatenate(parts, axis=0)
    hidden_ref[...] = hidden
    scaled = hidden * gain_ref[...]
    target = target_ref[...].astype(f32)
    lane = lax.broadcasted_iota(jnp.int32, sums_ref.shape, 1)
    sums = jnp.zeros(sums_ref.shape, f32)
    terms = (hidden * hidden, scaled * scaled, scaled * target, target * target)
    for i, term in enumerate(terms):
        sums = jnp.where(lane == i, jnp.sum(term, axis=1, keepdims=True), sums)
    sums_ref[...] = sums


def sum_rows(place, parts, own, arrived, gain, target):
    rows, units = target.shape
    early = [array for array, _, _ in parts if array is not None]
    ranges = [(array is not None, start, size) for array, start, size in parts]
    return pl.pallas_call(
        functools.partial(rows_kernel, ranges, len(arrived)),
        grid=(1,),
        in_specs=[SMEM, whole(gain.shape), whole(target.shape)]
        + [whole(own.shape)] * (1 + len(arrived))
        + [whole(array.shape) for array in early],
        out_specs=[whole((rows, units)), whole((rows, 128))],
        out_shape=[
            jax.ShapeDtypeStruct((rows, units), f32),
            jax.ShapeDtypeStruct((rows, 128), f32),
        ],
        compiler_params=params(12),
        cost_estimate=cost(),
        name="sum_rows",
    )(place, gain, target, own, *arrived, *early)


def gradient_kernel(all_units, place_ref, hidden_ref, gain_ref, target_ref, share_ref, *refs):
    all_sums, grads = refs[:-PARTS], refs[-PARTS:]
    rows = hidden_ref.shape[0]
    sums = jnp.concatenate(
        [
            sum(ref[(block ^ k) * ROWS : ((block ^ k) + 1) * ROWS, :] for k, ref in enumerate(all_sums))
            for block in range(rows // ROWS)
        ],
        axis=0,
    )
    squares, scaled_squares = sums[:, 0:1], sums[:, 1:2]
    products, target_squares = sums[:, 2:3], sums[:, 3:4]
    share = share_ref[:, 0:1]
    inverse_rms = lax.rsqrt(squares / all_units + epsilon)
    coupling = share * (inverse_rms * scaled_squares - products)
    loss = inverse_rms * (inverse_rms * scaled_squares - 2.0 * products) + target_squares
    loss = jnp.broadcast_to(jnp.sum(0.5 * share * loss, axis=0, keepdims=True), (loss.shape[0], 128))
    first = loss.astype(bf16)
    second = (loss - first.astype(f32)).astype(bf16)
    third = (loss - first.astype(f32) - second.astype(f32)).astype(bf16)
    lane = lax.broadcasted_iota(jnp.int32, loss.shape, 1)
    third = jnp.where(lane == 2, third.astype(f32), 0.0)
    loss = jnp.where(lane == 1, second.astype(f32), third)
    loss = jnp.where(lane == 0, first.astype(f32), loss).astype(bf16)
    hidden = hidden_ref[...]
    gain = gain_ref[...]
    residual = share * (hidden * inverse_rms * gain - target_ref[...].astype(f32))
    grad = inverse_rms * gain * residual - hidden * (inverse_rms**3 * coupling / all_units)
    width = hidden.shape[1] // PARTS
    for i, grad_ref in enumerate(grads):
        grad_ref[:, :width] = grad[:, i * width : (i + 1) * width].astype(bf16)
        if i == 0:
            grad_ref[:, width:] = loss


def gradient(place, hidden, all_sums, gain, target, share, all_units):
    rows, units = hidden.shape
    shapes = [(rows, units // PARTS + (128 if i == 0 else 0)) for i in range(PARTS)]
    return pl.pallas_call(
        functools.partial(gradient_kernel, all_units),
        grid=(1,),
        in_specs=[SMEM, whole(hidden.shape), whole(gain.shape), whole(hidden.shape)]
        + [whole((rows, 128))] * (1 + len(all_sums)),
        out_specs=[whole(shape) for shape in shapes],
        out_shape=[jax.ShapeDtypeStruct(shape, bf16) for shape in shapes],
        compiler_params=params(12),
        cost_estimate=cost(),
        name="gradient",
    )(place, hidden, gain, target, share, *all_sums)


def piece_copies(place_ref, pieces, target, sems):
    core, plane = place_ref[0], place_ref[1]
    slots = len(pieces) // 2
    copies = []
    for i, piece in enumerate(pieces):
        owner = (plane ^ (i % slots)) * 2 + (core if i < slots else 1 - core)
        copies.append(
            pltpu.make_async_copy(piece, target.at[:, owner], sems.at[i])
        )
    return copies


def by_block(pieces):
    return in_hbm(*[piece.reshape(piece.shape[0] // ROWS, ROWS, -1) for piece in pieces])


def backward_kernel(part_count, piece_count, place_ref, *refs):
    parts, refs = refs[:part_count], refs[part_count:]
    pieces, refs = refs[:piece_count], refs[piece_count:]
    rows_ref, sems = refs[-2:]
    out_ref, *loss = refs[-4:-2] if refs[-3].shape[-1] == 128 else refs[-3:-2]
    units = out_ref.shape[-1]

    @pl.when(pl.program_id(0) == 0)
    def _():
        run_copies(piece_copies(place_ref, pieces, rows_ref, sems))
        for loss_ref in loss:
            total = jnp.zeros(loss_ref.shape, f32)
            for owner in range(rows_ref.shape[1]):
                total += rows_ref[0, owner, :, units:].astype(f32)
            loss_ref[...] = total

    left = jnp.concatenate([part[...] for part in parts], axis=0)
    out_ref[...] = lax.dot_general(
        left,
        rows_ref[..., :units].reshape(left.shape[0], units),
        (((0,), (0,)), ((), ())),
        preferred_element_type=f32,
    ).astype(bf16)


def backward(place, parts, pieces, index, units, result=None):
    depth = parts[0].shape[1]
    tile = min(depth, 1024)
    width = units // PARTS
    blocks = pieces[0].shape[0] // ROWS
    operands = [place, *in_hbm(*parts), *by_block(pieces)]
    first = result is None
    out = pl.pallas_call(
        functools.partial(backward_kernel, len(parts), len(pieces)),
        grid=(depth // tile,),
        in_specs=[SMEM]
        + [pl.BlockSpec((part.shape[0], tile), lambda k: (0, k)) for part in parts]
        + [HBM] * (len(pieces) + (not first)),
        out_specs=[pl.BlockSpec((tile, width), lambda k: (k, index))]
        + [pl.BlockSpec((ROWS, 128), lambda k: (0, 0))] * first,
        out_shape=[jax.ShapeDtypeStruct((depth, units), bf16)]
        + [jax.ShapeDtypeStruct((ROWS, 128), f32)] * first,
        scratch_shapes=[
            pltpu.VMEM((blocks, len(pieces), ROWS, pieces[0].shape[1]), bf16),
            pltpu.SemaphoreType.DMA((len(pieces),)),
        ],
        input_output_aliases={} if first else {len(operands): 0},
        compiler_params=params(24),
        cost_estimate=cost(),
        name="backward",
    )(*operands, *([] if first else [result]))
    return out if first else [out[0], None]


def shards(features, weight, norm_gain, target, counts):
    groups, tp = lax.axis_size("grp"), lax.axis_size("tp")
    group, place_tp = lax.axis_index("grp"), lax.axis_index("tp")
    core, plane = place_tp % 2, place_tp // 2
    slots = tp // 2
    place = jnp.stack([core, plane, group]).astype(jnp.int32)
    group_rows = features.shape[0]
    all_units = norm_gain.shape[0] * groups
    gain = norm_gain[None, :]
    span = ROWS * tp
    sets = range(group_rows // span)

    accepted = jnp.sum(counts).astype(f32)
    blocks = group ^ jnp.arange(groups, dtype=jnp.int32)
    index = (
        jnp.arange(len(sets), dtype=jnp.int32)[:, None, None] * span
        + blocks[None, :, None] * group_rows
        + (plane * 2 + core) * ROWS
        + jnp.arange(ROWS, dtype=jnp.int32)[None, None, :]
    ).reshape(len(sets), groups * ROWS)
    live = (index % SPEC < jnp.take(counts, index // SPEC)).astype(f32) / accepted
    share = jnp.broadcast_to(live.reshape(-1, 1), (live.size, 128))

    last = [place]

    def turn(*waits):
        return after(place, *last, *waits)

    def ran(outputs):
        last[:] = jax.tree.leaves(outputs)
        return outputs

    own = ran(copy_rows(turn(), [(features, i * span, span) for i in sets]))
    block_rows = [{0: [own[i]]} for i in sets]
    for i in sets:
        if groups == 4:
            block_rows[i][1] = [exchange(own[i], "grp", 1)]
            block_rows[i][2] = [exchange(own[i], "grp", 2)]
        else:
            mask = 1
            while mask < groups:
                for block in range(mask):
                    block_rows[i][block ^ mask] = [exchange(block_rows[i][block][0], "grp", mask)]
                mask *= 2

    def send_corner(i):
        (first,), (second,) = block_rows[i][1], block_rows[i][2]
        half = span // 2
        low, high = ran(copy_rows(turn(first, second), [(first, 0, half), (second, half, half)]))
        block_rows[i][3] = [exchange(low, "grp", 2), exchange(high, "grp", 1)]

    def multiply(pieces):
        rows = [block_rows[i][block] for i, block in pieces]
        keep, send = ran(
            forward(turn(*[part for parts in rows for part in parts]), rows, weight_here, slots)
        )
        return keep, send

    def add_pair(*events):
        events = [(keep, exchange(after(send, *last), "tp", 1)) for keep, send in events]
        own_sum, out = ran(sum_pair(turn(*[arrived for _, arrived in events]), events))
        return own_sum, [exchange(value, "tp", 2 * k) for k, value in enumerate(out, 1)]

    def add_planes(own_sum, arrived):
        return ran(sum_planes(turn(*arrived), own_sum, arrived))

    def add_rows(early, own_sum, arrived):
        hidden, part = ran(sum_rows(turn(*arrived), early, own_sum, arrived, gain, targets))
        return hidden, [part] + [exchange(part, "grp", mask) for mask in range(1, groups)]

    def differentiate(hidden, sums):
        return ran(gradient(turn(*sums), hidden, sums, gain, targets, share, all_units))

    def spread(grad, *waits):
        grad = after(grad, *waits)
        return [grad] + [exchange(grad, "tp", 2 * k) for k in range(1, slots)]

    def spread_pair(pieces, *waits):
        return pieces + [exchange(after(value, *waits), "tp", 1) for value in pieces]

    weight_here = load(turn(), weight)
    targets = ran(take_targets(turn(share), target, group_rows, len(sets), groups))
    own_pair = multiply([(i, 0) for i in sets])
    own_planes = add_pair(own_pair)
    if groups == 4 and len(sets) == 2:
        send_corner(0)
        edge0 = multiply([(0, 1), (0, 2)])
        own_hidden = add_planes(*own_planes)
        edge0 = add_pair(edge0)
        send_corner(1)
        edge1 = multiply([(1, 1), (1, 2)])
        hidden0 = add_planes(*edge0)
        edge1 = add_pair(edge1)
        corner0 = multiply([(0, 3)])
        corner1 = multiply([(1, 3)])
        hidden1 = add_planes(*edge1)
        early = [
            (own_hidden, 0, ROWS),
            (hidden0, 0, 2 * ROWS),
            (None, 0, ROWS),
            (own_hidden, ROWS, ROWS),
            (hidden1, 0, 2 * ROWS),
            (None, ROWS, ROWS),
        ]
        rows = add_rows(early, *add_pair(corner0, corner1))
    else:
        own_hidden = add_planes(*own_planes)
        early = []
        for i in sets:
            early.append((own_hidden, i * ROWS, ROWS))
            for block in range(1, groups):
                pair = add_pair(multiply([(i, block)]))
                if (i, block) != (sets[-1], groups - 1):
                    early.append((add_planes(*pair), 0, ROWS))
        rows = add_rows(early + [(None, 0, ROWS)], *pair)
    grads = differentiate(*rows)
    parts = [part for i in sets for block in range(groups) for part in block_rows[i][block]]
    planes = []
    for grad in grads:
        planes.append(spread(grad, *[pieces[1] for pieces in planes[-1:]]))
    result = loss = None
    for i, pieces in enumerate(planes):
        pieces = spread_pair(pieces, *([] if i == 0 else [loss]))
        result, total = backward(turn(*pieces), parts, pieces, i, gain.shape[1], result)
        loss = total if i == 0 else loss
        ran(loss)
    return (result, jnp.sum(loss[0]))


def solution(mesh):
    placed = (P("grp", "tp"), P("tp", "grp"), P("grp"), P(None, "grp"), P())
    return jax.shard_map(
        shards, mesh=mesh, in_specs=placed, out_specs=(P("tp", "grp"), P()), check_vma=False
    )
```

```python
import functools
import jax
import jax.numpy as jnp
from jax import lax
from jax.experimental import pallas as pl
from jax.experimental.pallas import tpu as pltpu
from jax.sharding import PartitionSpec as P

SPEC = 8
epsilon = 1e-06
MIB = 2**20
ROWS = 16
PARTS = 2
HBM = pl.BlockSpec(memory_space=pltpu.HBM)
SMEM = pl.BlockSpec(memory_space=pltpu.SMEM)
VMEM = pl.BlockSpec(memory_space=pltpu.VMEM)
bf16, f32 = jnp.bfloat16, jnp.float32


def exchange(value, axis, mask):
    size = lax.axis_size(axis)
    return lax.ppermute(value, axis, [(i, i ^ mask) for i in range(size)])


def in_hbm(*arrays):
    return [pltpu.with_memory_space_constraint(array, pltpu.HBM) for array in arrays]


def after(value, *others):
    return lax.optimization_barrier((value, *others))[0]


def whole(shape):
    return pl.BlockSpec(shape, lambda _: (0,) * len(shape))


def params(mib):
    return pltpu.CompilerParams(vmem_limit_bytes=mib * MIB)


def cost(flops=1024, moved=1024):
    return pl.CostEstimate(flops=flops, bytes_accessed=moved, transcendentals=0)


def run_copies(copies):
    for copy in copies:
        copy.start()
    for copy in copies:
        copy.wait()


def copy_kernel(ranges, place_ref, *refs):
    count = len(ranges)
    sources, targets, holds, sems = refs[:count], refs[count : 2 * count], refs[2 * count : -1], refs[-1]
    into = [
        pltpu.make_async_copy(source.at[pl.ds(start, size), :], hold, sems.at[0, i])
        for i, (source, hold, (start, size)) in enumerate(zip(sources, holds, ranges))
    ]
    out = [
        pltpu.make_async_copy(hold, target, sems.at[1, i])
        for i, (hold, target) in enumerate(zip(holds, targets))
    ]
    for copy in into:
        copy.start()
    for first, second in zip(into, out):
        first.wait()
        second.start()
    for copy in out:
        copy.wait()


def copy_rows(place, pieces):
    shapes = [((size, array.shape[1]), array.dtype) for array, _, size in pieces]
    return pl.pallas_call(
        functools.partial(copy_kernel, [(start, size) for _, start, size in pieces]),
        in_specs=[SMEM] + [HBM] * len(pieces),
        out_specs=[HBM] * len(pieces),
        out_shape=[pltpu.HBM(*shape) for shape in shapes],
        scratch_shapes=[pltpu.VMEM(*shape) for shape in shapes]
        + [pltpu.SemaphoreType.DMA((2, len(pieces)))],
        compiler_params=params(12),
        cost_estimate=cost(),
        name="copy_rows",
    )(place, *in_hbm(*[array for array, _, _ in pieces]))


def load_kernel(place_ref, source_ref, target_ref, sem):
    run_copies([pltpu.make_async_copy(source_ref, target_ref, sem)])


def load(place, array):
    held = pl.pallas_call(
        load_kernel,
        in_specs=[SMEM, HBM],
        out_specs=VMEM,
        out_shape=pltpu.VMEM(array.shape, array.dtype),
        scratch_shapes=[pltpu.SemaphoreType.DMA],
        compiler_params=params(12),
        cost_estimate=cost(),
        name="load",
    )(place, *in_hbm(array))
    return pltpu.with_memory_space_constraint(held, pltpu.VMEM)


def forward_kernel(pieces, tile, place_ref, *refs):
    parts = refs[:pieces]
    weight_ref, keep_out, send_out, rows_ref, keep_ref, send_ref, sems, out_sems = refs[pieces:]
    copies = []
    start = 0
    for i, part in enumerate(parts):
        size = part.shape[0]
        copies.append(pltpu.make_async_copy(part, rows_ref.at[pl.ds(start, size), :], sems.at[i]))
        start += size
    run_copies(copies)
    shape = keep_ref.shape[:-1]
    units = keep_ref.shape[-1]
    for column in range(0, units, tile):
        columns = slice(column, column + tile)
        product = jnp.dot(
            rows_ref[...], weight_ref[:, columns], preferred_element_type=f32
        ).reshape(*shape, tile)
        keep_ref[..., columns] = product
        send_ref[..., columns] = product.astype(bf16)
    core, plane = place_ref[0], place_ref[1]
    copies = []
    for slot in range(keep_out.shape[0]):
        owner = (plane ^ slot) * 2
        copies += [
            pltpu.make_async_copy(
                keep_ref.at[:, owner + core], keep_out.at[slot], out_sems.at[0, slot]
            ),
            pltpu.make_async_copy(
                send_ref.at[:, owner + 1 - core], send_out.at[slot], out_sems.at[1, slot]
            ),
        ]
    run_copies(copies)


def forward(place, blocks, weight, slots):
    depth, units = weight.shape
    parts = [part for block in blocks for part in block]
    total_rows = sum(part.shape[0] for part in parts)
    count = len(blocks)
    tile = min(units, 512)
    scratch = (count, 2 * slots, ROWS, units)
    shape = (slots, count, ROWS, units)
    keep, send = pl.pallas_call(
        functools.partial(forward_kernel, len(parts), tile),
        in_specs=[SMEM] + [HBM] * len(parts) + [VMEM],
        out_specs=[HBM, HBM],
        out_shape=[pltpu.HBM(shape, f32), pltpu.HBM(shape, bf16)],
        scratch_shapes=[
            pltpu.VMEM((total_rows, depth), bf16),
            pltpu.VMEM(scratch, f32),
            pltpu.VMEM(scratch, bf16),
            pltpu.SemaphoreType.DMA((len(parts),)),
            pltpu.SemaphoreType.DMA((2, slots)),
        ],
        compiler_params=params(12),
        cost_estimate=cost(),
        name="forward",
    )(place, *in_hbm(*parts), weight)
    shape = (slots, count * ROWS, units)
    return keep.reshape(shape), send.reshape(shape)


def pair_kernel(count, place_ref, *refs):
    keeps, arrived = refs[:count], refs[count : 2 * count]
    own_ref, *sends = refs[2 * count :]
    start = 0
    for keep_ref, arrived_ref in zip(keeps, arrived):
        rows = pl.ds(start, keep_ref.shape[1])
        own_ref[rows, :] = keep_ref[0] + arrived_ref[0].astype(f32)
        for k, send_ref in enumerate(sends, 1):
            send_ref[rows, :] = (keep_ref[k] + arrived_ref[k].astype(f32)).astype(bf16)
        start += keep_ref.shape[1]


def sum_pair(place, events):
    keeps, arrived = zip(*events)
    slots, _, units = keeps[0].shape
    rows = sum(keep.shape[1] for keep in keeps)
    out = pl.pallas_call(
        functools.partial(pair_kernel, len(keeps)),
        grid=(1,),
        in_specs=[SMEM] + [whole(keep.shape) for keep in keeps] * 2,
        out_specs=[whole((rows, units))] * slots,
        out_shape=[jax.ShapeDtypeStruct((rows, units), f32)]
        + [jax.ShapeDtypeStruct((rows, units), bf16)] * (slots - 1),
        compiler_params=params(12),
        cost_estimate=cost(),
        name="sum_pair",
    )(place, *keeps, *arrived)
    return out[0], out[1:]


def planes_kernel(place_ref, own_ref, *refs):
    arrived, hidden_ref = refs[:-1], refs[-1]
    hidden = own_ref[...]
    for value in arrived:
        hidden = hidden + value[...].astype(f32)
    hidden_ref[...] = hidden


def sum_planes(place, own, arrived):
    return pl.pallas_call(
        planes_kernel,
        grid=(1,),
        in_specs=[SMEM] + [whole(own.shape)] * (1 + len(arrived)),
        out_specs=whole(own.shape),
        out_shape=jax.ShapeDtypeStruct(own.shape, f32),
        compiler_params=params(12),
        cost_estimate=cost(),
        name="sum_planes",
    )(place, own, *arrived)


def targets_kernel(group_rows, sets, groups, place_ref, target_ref, out_ref, hold_ref, sems):
    core, plane, group = place_ref[0], place_ref[1], place_ref[2]
    span = group_rows // sets
    copies = []
    for i in range(sets):
        for block in range(groups):
            row = (group ^ block) * group_rows + i * span + (plane * 2 + core) * ROWS
            copies.append(
                pltpu.make_async_copy(
                    target_ref.at[pl.ds(pl.multiple_of(row, ROWS), ROWS), :],
                    hold_ref.at[pl.ds((i * groups + block) * ROWS, ROWS), :],
                    sems.at[i * groups + block],
                )
            )
    run_copies(copies)
    run_copies([pltpu.make_async_copy(hold_ref, out_ref, sems.at[sets * groups])])


def take_targets(place, target, group_rows, sets, groups):
    shape = (sets * groups * ROWS, target.shape[1])
    return pl.pallas_call(
        functools.partial(targets_kernel, group_rows, sets, groups),
        in_specs=[SMEM, HBM],
        out_specs=HBM,
        out_shape=pltpu.HBM(shape, bf16),
        scratch_shapes=[
            pltpu.VMEM(shape, bf16),
            pltpu.SemaphoreType.DMA((sets * groups + 1,)),
        ],
        compiler_params=params(12),
        cost_estimate=cost(),
        name="take_targets",
    )(place, *in_hbm(target))


def rows_kernel(ranges, late, place_ref, gain_ref, target_ref, *refs):
    own_ref, *arrived = refs[: 1 + late]
    early, (hidden_ref, sums_ref) = list(refs[1 + late : -2]), refs[-2:]
    last = own_ref[...]
    for value in arrived:
        last = last + value[...].astype(f32)
    parts = []
    for is_early, start, size in ranges:
        part = early.pop(0)[...] if is_early else last
        parts.append(part[start : start + size, :])
    hidden = jnp.concatenate(parts, axis=0)
    hidden_ref[...] = hidden
    scaled = hidden * gain_ref[...]
    target = target_ref[...].astype(f32)
    lane = lax.broadcasted_iota(jnp.int32, sums_ref.shape, 1)
    sums = jnp.zeros(sums_ref.shape, f32)
    terms = (hidden * hidden, scaled * scaled, scaled * target, target * target)
    for i, term in enumerate(terms):
        sums = jnp.where(lane == i, jnp.sum(term, axis=1, keepdims=True), sums)
    sums_ref[...] = sums


def sum_rows(place, parts, own, arrived, gain, target):
    rows, units = target.shape
    early = [array for array, _, _ in parts if array is not None]
    ranges = [(array is not None, start, size) for array, start, size in parts]
    return pl.pallas_call(
        functools.partial(rows_kernel, ranges, len(arrived)),
        grid=(1,),
        in_specs=[SMEM, whole(gain.shape), whole(target.shape)]
        + [whole(own.shape)] * (1 + len(arrived))
        + [whole(array.shape) for array in early],
        out_specs=[whole((rows, units)), whole((rows, 128))],
        out_shape=[
            jax.ShapeDtypeStruct((rows, units), f32),
            jax.ShapeDtypeStruct((rows, 128), f32),
        ],
        compiler_params=params(12),
        cost_estimate=cost(),
        name="sum_rows",
    )(place, gain, target, own, *arrived, *early)


def gradient_kernel(all_units, place_ref, hidden_ref, gain_ref, target_ref, share_ref, *refs):
    all_sums, grads = refs[:-PARTS], refs[-PARTS:]
    rows = hidden_ref.shape[0]
    sums = jnp.concatenate(
        [
            sum(ref[(block ^ k) * ROWS : ((block ^ k) + 1) * ROWS, :] for k, ref in enumerate(all_sums))
            for block in range(rows // ROWS)
        ],
        axis=0,
    )
    squares, scaled_squares = sums[:, 0:1], sums[:, 1:2]
    products, target_squares = sums[:, 2:3], sums[:, 3:4]
    share = share_ref[:, 0:1]
    inverse_rms = lax.rsqrt(squares / all_units + epsilon)
    coupling = share * (inverse_rms * scaled_squares - products)
    loss = inverse_rms * (inverse_rms * scaled_squares - 2.0 * products) + target_squares
    loss = jnp.broadcast_to(jnp.sum(0.5 * share * loss, axis=0, keepdims=True), (loss.shape[0], 128))
    first = loss.astype(bf16)
    second = (loss - first.astype(f32)).astype(bf16)
    third = (loss - first.astype(f32) - second.astype(f32)).astype(bf16)
    lane = lax.broadcasted_iota(jnp.int32, loss.shape, 1)
    third = jnp.where(lane == 2, third.astype(f32), 0.0)
    loss = jnp.where(lane == 1, second.astype(f32), third)
    loss = jnp.where(lane == 0, first.astype(f32), loss).astype(bf16)
    hidden = hidden_ref[...]
    gain = gain_ref[...]
    residual = share * (hidden * inverse_rms * gain - target_ref[...].astype(f32))
    grad = inverse_rms * gain * residual - hidden * (inverse_rms**3 * coupling / all_units)
    width = hidden.shape[1] // PARTS
    for i, grad_ref in enumerate(grads):
        grad_ref[:, :width] = grad[:, i * width : (i + 1) * width].astype(bf16)
        if i == 0:
            grad_ref[:, width:] = loss


def gradient(place, hidden, all_sums, gain, target, share, all_units):
    rows, units = hidden.shape
    shapes = [(rows, units // PARTS + (128 if i == 0 else 0)) for i in range(PARTS)]
    return pl.pallas_call(
        functools.partial(gradient_kernel, all_units),
        grid=(1,),
        in_specs=[SMEM, whole(hidden.shape), whole(gain.shape), whole(hidden.shape)]
        + [whole((rows, 128))] * (1 + len(all_sums)),
        out_specs=[whole(shape) for shape in shapes],
        out_shape=[jax.ShapeDtypeStruct(shape, bf16) for shape in shapes],
        compiler_params=params(12),
        cost_estimate=cost(),
        name="gradient",
    )(place, hidden, gain, target, share, *all_sums)


def place_pieces(place_ref, pieces, rows_ref):
    core, plane = place_ref[0], place_ref[1]
    slots = len(pieces) // 2
    for i, piece in enumerate(pieces):
        owner = (plane ^ (i % slots)) * 2 + (core if i < slots else 1 - core)
        rows_ref[:, owner] = piece[...]


def by_block(pieces):
    return in_hbm(*[piece.reshape(piece.shape[0] // ROWS, ROWS, -1) for piece in pieces])


def backward_kernel(part_count, piece_count, place_ref, *refs):
    parts, refs = refs[:part_count], refs[part_count:]
    pieces, refs = refs[:piece_count], refs[piece_count:]
    rows_ref = refs[-1]
    out_ref, *loss = refs[-3:-1] if refs[-2].shape[-1] == 1 else refs[-2:-1]
    units = out_ref.shape[-1]

    @pl.when(pl.program_id(0) == 0)
    def _():
        place_pieces(place_ref, pieces, rows_ref)
        for loss_ref in loss:
            total = jnp.zeros((ROWS, 128), f32)
            for owner in range(rows_ref.shape[1]):
                total += rows_ref[0, owner, :, units:].astype(f32)
            loss_ref[0, 0] = jnp.sum(total[:1])

    left = jnp.concatenate([part[...] for part in parts], axis=0)
    out_ref[...] = lax.dot_general(
        left,
        rows_ref[..., :units].reshape(left.shape[0], units),
        (((0,), (0,)), ((), ())),
        preferred_element_type=f32,
    ).astype(bf16)


def backward(place, parts, pieces, index, units, result=None):
    depth = parts[0].shape[1]
    tile = min(depth, 1024)
    width = units // PARTS
    blocks = pieces[0].shape[0] // ROWS
    here = by_block(pieces)
    operands = [place, *in_hbm(*parts), *here]
    first = result is None
    out = pl.pallas_call(
        functools.partial(backward_kernel, len(parts), len(pieces)),
        grid=(depth // tile,),
        in_specs=[SMEM]
        + [pl.BlockSpec((part.shape[0], tile), lambda k: (0, k)) for part in parts]
        + [whole(piece.shape) for piece in here]
        + [HBM] * (not first),
        out_specs=[pl.BlockSpec((tile, width), lambda k: (k, index))]
        + [SMEM] * first,
        out_shape=[jax.ShapeDtypeStruct((depth, units), bf16)]
        + [jax.ShapeDtypeStruct((1, 1), f32)] * first,
        scratch_shapes=[
            pltpu.VMEM((blocks, len(pieces), ROWS, pieces[0].shape[1]), bf16),
        ],
        input_output_aliases={} if first else {len(operands): 0},
        compiler_params=params(24),
        cost_estimate=cost(),
        name="backward",
    )(*operands, *([] if first else [result]))
    return out if first else [out[0], None]


def shards(features, weight, norm_gain, target, counts):
    groups, tp = lax.axis_size("grp"), lax.axis_size("tp")
    group, place_tp = lax.axis_index("grp"), lax.axis_index("tp")
    core, plane = place_tp % 2, place_tp // 2
    slots = tp // 2
    place = jnp.stack([core, plane, group]).astype(jnp.int32)
    group_rows = features.shape[0]
    all_units = norm_gain.shape[0] * groups
    gain = norm_gain[None, :]
    span = ROWS * tp
    sets = range(group_rows // span)

    accepted = jnp.sum(counts).astype(f32)
    blocks = group ^ jnp.arange(groups, dtype=jnp.int32)
    index = (
        jnp.arange(len(sets), dtype=jnp.int32)[:, None, None] * span
        + blocks[None, :, None] * group_rows
        + (plane * 2 + core) * ROWS
        + jnp.arange(ROWS, dtype=jnp.int32)[None, None, :]
    ).reshape(len(sets), groups * ROWS)
    live = (index % SPEC < jnp.take(counts, index // SPEC)).astype(f32) / accepted
    share = jnp.broadcast_to(live.reshape(-1, 1), (live.size, 128))

    last = [place]

    def turn(*waits):
        return after(place, *last, *waits)

    def ran(outputs):
        last[:] = jax.tree.leaves(outputs)
        return outputs

    own = ran(copy_rows(turn(), [(features, i * span, span) for i in sets]))
    block_rows = [{0: [own[i]]} for i in sets]
    for i in sets:
        if groups == 4:
            block_rows[i][1] = [exchange(own[i], "grp", 1)]
            block_rows[i][2] = [exchange(own[i], "grp", 2)]
        else:
            mask = 1
            while mask < groups:
                for block in range(mask):
                    block_rows[i][block ^ mask] = [exchange(block_rows[i][block][0], "grp", mask)]
                mask *= 2

    def send_corner(i):
        (first,), (second,) = block_rows[i][1], block_rows[i][2]
        half = span // 2
        low, high = ran(copy_rows(turn(first, second), [(first, 0, half), (second, half, half)]))
        block_rows[i][3] = [exchange(low, "grp", 2), exchange(high, "grp", 1)]

    def multiply(pieces):
        rows = [block_rows[i][block] for i, block in pieces]
        keep, send = ran(
            forward(turn(*[part for parts in rows for part in parts]), rows, weight_here, slots)
        )
        return keep, send

    def add_pair(*events):
        events = [(keep, exchange(after(send, *last), "tp", 1)) for keep, send in events]
        own_sum, out = ran(sum_pair(turn(*[arrived for _, arrived in events]), events))
        return own_sum, [exchange(value, "tp", 2 * k) for k, value in enumerate(out, 1)]

    def add_planes(own_sum, arrived):
        return ran(sum_planes(turn(*arrived), own_sum, arrived))

    def add_rows(early, own_sum, arrived):
        hidden, part = ran(sum_rows(turn(*arrived), early, own_sum, arrived, gain, targets))
        return hidden, [part] + [exchange(part, "grp", mask) for mask in range(1, groups)]

    def differentiate(hidden, sums):
        return ran(gradient(turn(*sums), hidden, sums, gain, targets, share, all_units))

    def spread(grad, *waits):
        grad = after(grad, *waits)
        return [grad] + [exchange(grad, "tp", 2 * k) for k in range(1, slots)]

    def spread_pair(pieces, *waits):
        return pieces + [exchange(after(value, *waits), "tp", 1) for value in pieces]

    weight_here = load(turn(), weight)
    targets = ran(take_targets(turn(share), target, group_rows, len(sets), groups))
    own_pair = multiply([(i, 0) for i in sets])
    own_planes = add_pair(own_pair)
    if groups == 4 and len(sets) == 2:
        send_corner(0)
        edge0 = multiply([(0, 1), (0, 2)])
        own_hidden = add_planes(*own_planes)
        edge0 = add_pair(edge0)
        send_corner(1)
        edge1 = multiply([(1, 1), (1, 2)])
        hidden0 = add_planes(*edge0)
        edge1 = add_pair(edge1)
        corner0 = multiply([(0, 3)])
        corner1 = multiply([(1, 3)])
        hidden1 = add_planes(*edge1)
        early = [
            (own_hidden, 0, ROWS),
            (hidden0, 0, 2 * ROWS),
            (None, 0, ROWS),
            (own_hidden, ROWS, ROWS),
            (hidden1, 0, 2 * ROWS),
            (None, ROWS, ROWS),
        ]
        rows = add_rows(early, *add_pair(corner0, corner1))
    else:
        own_hidden = add_planes(*own_planes)
        early = []
        for i in sets:
            early.append((own_hidden, i * ROWS, ROWS))
            for block in range(1, groups):
                pair = add_pair(multiply([(i, block)]))
                if (i, block) != (sets[-1], groups - 1):
                    early.append((add_planes(*pair), 0, ROWS))
        rows = add_rows(early + [(None, 0, ROWS)], *pair)
    grads = differentiate(*rows)
    parts = [part for i in sets for block in range(groups) for part in block_rows[i][block]]
    planes = []
    for grad in grads:
        planes.append(spread(grad, *[pieces[1] for pieces in planes[-1:]]))
    result = loss = None
    for i, pieces in enumerate(planes):
        pieces = spread_pair(pieces, *([] if i == 0 else [loss]))
        result, total = backward(turn(*pieces), parts, pieces, i, gain.shape[1], result)
        loss = total if i == 0 else loss
        ran(loss)
    return (result, loss.reshape(()))


def solution(mesh):
    placed = (P("grp", "tp"), P("tp", "grp"), P("grp"), P(None, "grp"), P())
    return jax.shard_map(
        shards, mesh=mesh, in_specs=placed, out_specs=(P("tp", "grp"), P()), check_vma=False
    )
```

```python
import functools
import jax
import jax.numpy as jnp
from jax import lax
from jax.experimental import pallas as pl
from jax.experimental.pallas import tpu as pltpu
from jax.sharding import PartitionSpec as P

SPEC = 8
epsilon = 1e-06
MIB = 2**20
ROWS = 16
PARTS = 2
HBM = pl.BlockSpec(memory_space=pltpu.HBM)
SMEM = pl.BlockSpec(memory_space=pltpu.SMEM)
VMEM = pl.BlockSpec(memory_space=pltpu.VMEM)
bf16, f32 = jnp.bfloat16, jnp.float32


def exchange(value, axis, mask):
    size = lax.axis_size(axis)
    return lax.ppermute(value, axis, [(i, i ^ mask) for i in range(size)])


def in_hbm(*arrays):
    return [pltpu.with_memory_space_constraint(array, pltpu.HBM) for array in arrays]


def after(value, *others):
    return lax.optimization_barrier((value, *others))[0]


def whole(shape):
    return pl.BlockSpec(shape, lambda _: (0,) * len(shape))


def params(mib):
    return pltpu.CompilerParams(vmem_limit_bytes=mib * MIB)


def cost(flops=1024, moved=1024):
    return pl.CostEstimate(flops=flops, bytes_accessed=moved, transcendentals=0)


def run_copies(copies):
    for copy in copies:
        copy.start()
    for copy in copies:
        copy.wait()


def copy_kernel(ranges, place_ref, *refs):
    count = len(ranges)
    sources, targets, holds, sems = refs[:count], refs[count : 2 * count], refs[2 * count : -1], refs[-1]
    into = [
        pltpu.make_async_copy(source.at[pl.ds(start, size), :], hold, sems.at[0, i])
        for i, (source, hold, (start, size)) in enumerate(zip(sources, holds, ranges))
    ]
    out = [
        pltpu.make_async_copy(hold, target, sems.at[1, i])
        for i, (hold, target) in enumerate(zip(holds, targets))
    ]
    for copy in into:
        copy.start()
    for first, second in zip(into, out):
        first.wait()
        second.start()
    for copy in out:
        copy.wait()


def copy_rows(place, pieces):
    shapes = [((size, array.shape[1]), array.dtype) for array, _, size in pieces]
    return pl.pallas_call(
        functools.partial(copy_kernel, [(start, size) for _, start, size in pieces]),
        in_specs=[SMEM] + [HBM] * len(pieces),
        out_specs=[HBM] * len(pieces),
        out_shape=[pltpu.HBM(*shape) for shape in shapes],
        scratch_shapes=[pltpu.VMEM(*shape) for shape in shapes]
        + [pltpu.SemaphoreType.DMA((2, len(pieces)))],
        compiler_params=params(12),
        cost_estimate=cost(),
        name="copy_rows",
    )(place, *in_hbm(*[array for array, _, _ in pieces]))


def load_kernel(place_ref, source_ref, target_ref, sem):
    run_copies([pltpu.make_async_copy(source_ref, target_ref, sem)])


def load(place, array):
    held = pl.pallas_call(
        load_kernel,
        in_specs=[SMEM, HBM],
        out_specs=VMEM,
        out_shape=pltpu.VMEM(array.shape, array.dtype),
        scratch_shapes=[pltpu.SemaphoreType.DMA],
        compiler_params=params(12),
        cost_estimate=cost(),
        name="load",
    )(place, *in_hbm(array))
    return pltpu.with_memory_space_constraint(held, pltpu.VMEM)


def forward_kernel(pieces, tile, place_ref, *refs):
    parts = refs[:pieces]
    weight_ref, keep_out, send_out, rows_ref, keep_ref, send_ref, sems, out_sems = refs[pieces:]
    copies = []
    start = 0
    for i, part in enumerate(parts):
        size = part.shape[0]
        copies.append(pltpu.make_async_copy(part, rows_ref.at[pl.ds(start, size), :], sems.at[i]))
        start += size
    run_copies(copies)
    shape = keep_ref.shape[:-1]
    units = keep_ref.shape[-1]
    for column in range(0, units, tile):
        columns = slice(column, column + tile)
        product = jnp.dot(
            rows_ref[...], weight_ref[:, columns], preferred_element_type=f32
        ).reshape(*shape, tile)
        keep_ref[..., columns] = product
        send_ref[..., columns] = product.astype(bf16)
    core, plane = place_ref[0], place_ref[1]
    copies = []
    for slot in range(keep_out.shape[0]):
        owner = (plane ^ slot) * 2
        copies += [
            pltpu.make_async_copy(
                keep_ref.at[:, owner + core], keep_out.at[slot], out_sems.at[0, slot]
            ),
            pltpu.make_async_copy(
                send_ref.at[:, owner + 1 - core], send_out.at[slot], out_sems.at[1, slot]
            ),
        ]
    run_copies(copies)


def forward(place, blocks, weight, slots):
    depth, units = weight.shape
    parts = [part for block in blocks for part in block]
    total_rows = sum(part.shape[0] for part in parts)
    count = len(blocks)
    tile = min(units, 512)
    scratch = (count, 2 * slots, ROWS, units)
    shape = (slots, count, ROWS, units)
    keep, send = pl.pallas_call(
        functools.partial(forward_kernel, len(parts), tile),
        in_specs=[SMEM] + [pl.BlockSpec(memory_space=pl.ANY)] * len(parts) + [VMEM],
        out_specs=[HBM, HBM],
        out_shape=[pltpu.HBM(shape, f32), pltpu.HBM(shape, bf16)],
        scratch_shapes=[
            pltpu.VMEM((total_rows, depth), bf16),
            pltpu.VMEM(scratch, f32),
            pltpu.VMEM(scratch, bf16),
            pltpu.SemaphoreType.DMA((len(parts),)),
            pltpu.SemaphoreType.DMA((2, slots)),
        ],
        compiler_params=params(12),
        cost_estimate=cost(),
        name="forward",
    )(place, *(parts if total_rows <= 128 else in_hbm(*parts)), weight)
    shape = (slots, count * ROWS, units)
    return keep.reshape(shape), send.reshape(shape)


def pair_kernel(count, place_ref, *refs):
    keeps, arrived = refs[:count], refs[count : 2 * count]
    own_ref, *sends = refs[2 * count :]
    start = 0
    for keep_ref, arrived_ref in zip(keeps, arrived):
        rows = pl.ds(start, keep_ref.shape[1])
        own_ref[rows, :] = keep_ref[0] + arrived_ref[0].astype(f32)
        for k, send_ref in enumerate(sends, 1):
            send_ref[rows, :] = (keep_ref[k] + arrived_ref[k].astype(f32)).astype(bf16)
        start += keep_ref.shape[1]


def sum_pair(place, events):
    keeps, arrived = zip(*events)
    slots, _, units = keeps[0].shape
    rows = sum(keep.shape[1] for keep in keeps)
    out = pl.pallas_call(
        functools.partial(pair_kernel, len(keeps)),
        grid=(1,),
        in_specs=[SMEM] + [whole(keep.shape) for keep in keeps] * 2,
        out_specs=[whole((rows, units))] * slots,
        out_shape=[jax.ShapeDtypeStruct((rows, units), f32)]
        + [jax.ShapeDtypeStruct((rows, units), bf16)] * (slots - 1),
        compiler_params=params(12),
        cost_estimate=cost(),
        name="sum_pair",
    )(place, *keeps, *arrived)
    return out[0], out[1:]


def planes_kernel(place_ref, own_ref, *refs):
    arrived, hidden_ref = refs[:-1], refs[-1]
    hidden = own_ref[...]
    for value in arrived:
        hidden = hidden + value[...].astype(f32)
    hidden_ref[...] = hidden


def sum_planes(place, own, arrived):
    return pl.pallas_call(
        planes_kernel,
        grid=(1,),
        in_specs=[SMEM] + [whole(own.shape)] * (1 + len(arrived)),
        out_specs=whole(own.shape),
        out_shape=jax.ShapeDtypeStruct(own.shape, f32),
        compiler_params=params(12),
        cost_estimate=cost(),
        name="sum_planes",
    )(place, own, *arrived)


def targets_kernel(group_rows, sets, groups, place_ref, target_ref, out_ref, hold_ref, sems):
    core, plane, group = place_ref[0], place_ref[1], place_ref[2]
    span = group_rows // sets
    copies = []
    for i in range(sets):
        for block in range(groups):
            row = (group ^ block) * group_rows + i * span + (plane * 2 + core) * ROWS
            copies.append(
                pltpu.make_async_copy(
                    target_ref.at[pl.ds(pl.multiple_of(row, ROWS), ROWS), :],
                    hold_ref.at[pl.ds((i * groups + block) * ROWS, ROWS), :],
                    sems.at[i * groups + block],
                )
            )
    run_copies(copies)
    run_copies([pltpu.make_async_copy(hold_ref, out_ref, sems.at[sets * groups])])


def take_targets(place, target, group_rows, sets, groups):
    shape = (sets * groups * ROWS, target.shape[1])
    return pl.pallas_call(
        functools.partial(targets_kernel, group_rows, sets, groups),
        in_specs=[SMEM, HBM],
        out_specs=HBM,
        out_shape=pltpu.HBM(shape, bf16),
        scratch_shapes=[
            pltpu.VMEM(shape, bf16),
            pltpu.SemaphoreType.DMA((sets * groups + 1,)),
        ],
        compiler_params=params(12),
        cost_estimate=cost(),
        name="take_targets",
    )(place, *in_hbm(target))


def rows_kernel(ranges, late, place_ref, gain_ref, target_ref, *refs):
    own_ref, *arrived = refs[: 1 + late]
    early, (hidden_ref, sums_ref) = list(refs[1 + late : -2]), refs[-2:]
    last = own_ref[...]
    for value in arrived:
        last = last + value[...].astype(f32)
    parts = []
    for is_early, start, size in ranges:
        part = early.pop(0)[...] if is_early else last
        parts.append(part[start : start + size, :])
    hidden = jnp.concatenate(parts, axis=0)
    hidden_ref[...] = hidden
    scaled = hidden * gain_ref[...]
    target = target_ref[...].astype(f32)
    lane = lax.broadcasted_iota(jnp.int32, sums_ref.shape, 1)
    sums = jnp.zeros(sums_ref.shape, f32)
    terms = (hidden * hidden, scaled * scaled, scaled * target, target * target)
    for i, term in enumerate(terms):
        sums = jnp.where(lane == i, jnp.sum(term, axis=1, keepdims=True), sums)
    sums_ref[...] = sums


def sum_rows(place, parts, own, arrived, gain, target):
    rows, units = target.shape
    early = [array for array, _, _ in parts if array is not None]
    ranges = [(array is not None, start, size) for array, start, size in parts]
    return pl.pallas_call(
        functools.partial(rows_kernel, ranges, len(arrived)),
        grid=(1,),
        in_specs=[SMEM, whole(gain.shape), whole(target.shape)]
        + [whole(own.shape)] * (1 + len(arrived))
        + [whole(array.shape) for array in early],
        out_specs=[whole((rows, units)), whole((rows, 128))],
        out_shape=[
            jax.ShapeDtypeStruct((rows, units), f32),
            jax.ShapeDtypeStruct((rows, 128), f32),
        ],
        compiler_params=params(12),
        cost_estimate=cost(),
        name="sum_rows",
    )(place, gain, target, own, *arrived, *early)


def gradient_kernel(all_units, place_ref, hidden_ref, gain_ref, target_ref, share_ref, *refs):
    all_sums, grads = refs[:-PARTS], refs[-PARTS:]
    rows = hidden_ref.shape[0]
    sums = jnp.concatenate(
        [
            sum(ref[(block ^ k) * ROWS : ((block ^ k) + 1) * ROWS, :] for k, ref in enumerate(all_sums))
            for block in range(rows // ROWS)
        ],
        axis=0,
    )
    squares, scaled_squares = sums[:, 0:1], sums[:, 1:2]
    products, target_squares = sums[:, 2:3], sums[:, 3:4]
    share = share_ref[:, 0:1]
    inverse_rms = lax.rsqrt(squares / all_units + epsilon)
    coupling = share * (inverse_rms * scaled_squares - products)
    loss = inverse_rms * (inverse_rms * scaled_squares - 2.0 * products) + target_squares
    loss = jnp.broadcast_to(jnp.sum(0.5 * share * loss, axis=0, keepdims=True), (loss.shape[0], 128))
    first = loss.astype(bf16)
    second = (loss - first.astype(f32)).astype(bf16)
    third = (loss - first.astype(f32) - second.astype(f32)).astype(bf16)
    lane = lax.broadcasted_iota(jnp.int32, loss.shape, 1)
    third = jnp.where(lane == 2, third.astype(f32), 0.0)
    loss = jnp.where(lane == 1, second.astype(f32), third)
    loss = jnp.where(lane == 0, first.astype(f32), loss).astype(bf16)
    hidden = hidden_ref[...]
    gain = gain_ref[...]
    residual = share * (hidden * inverse_rms * gain - target_ref[...].astype(f32))
    grad = inverse_rms * gain * residual - hidden * (inverse_rms**3 * coupling / all_units)
    width = hidden.shape[1] // PARTS
    for i, grad_ref in enumerate(grads):
        grad_ref[:, :width] = grad[:, i * width : (i + 1) * width].astype(bf16)
        if i == 0:
            grad_ref[:, width:] = loss


def gradient(place, hidden, all_sums, gain, target, share, all_units):
    rows, units = hidden.shape
    shapes = [(rows, units // PARTS + (128 if i == 0 else 0)) for i in range(PARTS)]
    return pl.pallas_call(
        functools.partial(gradient_kernel, all_units),
        grid=(1,),
        in_specs=[SMEM, whole(hidden.shape), whole(gain.shape), whole(hidden.shape)]
        + [whole((rows, 128))] * (1 + len(all_sums)),
        out_specs=[whole(shape) for shape in shapes],
        out_shape=[jax.ShapeDtypeStruct(shape, bf16) for shape in shapes],
        compiler_params=params(12),
        cost_estimate=cost(),
        name="gradient",
    )(place, hidden, gain, target, share, *all_sums)


def place_pieces(place_ref, pieces, rows_ref):
    core, plane = place_ref[0], place_ref[1]
    slots = len(pieces) // 2
    for i, piece in enumerate(pieces):
        owner = (plane ^ (i % slots)) * 2 + (core if i < slots else 1 - core)
        rows_ref[:, owner] = piece[...]


def by_block(pieces):
    return in_hbm(*[piece.reshape(piece.shape[0] // ROWS, ROWS, -1) for piece in pieces])


def backward_kernel(part_count, piece_count, place_ref, *refs):
    parts, refs = refs[:part_count], refs[part_count:]
    pieces, refs = refs[:piece_count], refs[piece_count:]
    rows_ref = refs[-1]
    out_ref, *loss = refs[-3:-1] if refs[-2].shape[-1] == 1 else refs[-2:-1]
    units = out_ref.shape[-1]

    @pl.when(pl.program_id(0) == 0)
    def _():
        place_pieces(place_ref, pieces, rows_ref)
        for loss_ref in loss:
            total = jnp.zeros((ROWS, 128), f32)
            for owner in range(rows_ref.shape[1]):
                total += rows_ref[0, owner, :, units:].astype(f32)
            loss_ref[0, 0] = jnp.sum(total[:1])

    left = jnp.concatenate([part[...] for part in parts], axis=0)
    out_ref[...] = lax.dot_general(
        left,
        rows_ref[..., :units].reshape(left.shape[0], units),
        (((0,), (0,)), ((), ())),
        preferred_element_type=f32,
    ).astype(bf16)


def backward(place, parts, pieces, index, units, result=None):
    depth = parts[0].shape[1]
    tile = min(depth, 1024)
    width = units // PARTS
    blocks = pieces[0].shape[0] // ROWS
    here = by_block(pieces)
    operands = [place, *in_hbm(*parts), *here]
    first = result is None
    out = pl.pallas_call(
        functools.partial(backward_kernel, len(parts), len(pieces)),
        grid=(depth // tile,),
        in_specs=[SMEM]
        + [pl.BlockSpec((part.shape[0], tile), lambda k: (0, k)) for part in parts]
        + [whole(piece.shape) for piece in here]
        + [HBM] * (not first),
        out_specs=[pl.BlockSpec((tile, width), lambda k: (k, index))]
        + [SMEM] * first,
        out_shape=[jax.ShapeDtypeStruct((depth, units), bf16)]
        + [jax.ShapeDtypeStruct((1, 1), f32)] * first,
        scratch_shapes=[
            pltpu.VMEM((blocks, len(pieces), ROWS, pieces[0].shape[1]), bf16),
        ],
        input_output_aliases={} if first else {len(operands): 0},
        compiler_params=params(24),
        cost_estimate=cost(),
        name="backward",
    )(*operands, *([] if first else [result]))
    return out if first else [out[0], None]


def shards(features, weight, norm_gain, target, counts):
    groups, tp = lax.axis_size("grp"), lax.axis_size("tp")
    group, place_tp = lax.axis_index("grp"), lax.axis_index("tp")
    core, plane = place_tp % 2, place_tp // 2
    slots = tp // 2
    place = jnp.stack([core, plane, group]).astype(jnp.int32)
    group_rows = features.shape[0]
    all_units = norm_gain.shape[0] * groups
    gain = norm_gain[None, :]
    span = ROWS * tp
    sets = range(group_rows // span)

    accepted = jnp.sum(counts).astype(f32)
    blocks = group ^ jnp.arange(groups, dtype=jnp.int32)
    index = (
        jnp.arange(len(sets), dtype=jnp.int32)[:, None, None] * span
        + blocks[None, :, None] * group_rows
        + (plane * 2 + core) * ROWS
        + jnp.arange(ROWS, dtype=jnp.int32)[None, None, :]
    ).reshape(len(sets), groups * ROWS)
    live = (index % SPEC < jnp.take(counts, index // SPEC)).astype(f32) / accepted
    share = jnp.broadcast_to(live.reshape(-1, 1), (live.size, 128))

    last = [place]

    def turn(*waits):
        return after(place, *last, *waits)

    def ran(outputs):
        last[:] = jax.tree.leaves(outputs)
        return outputs

    own = ran(copy_rows(turn(), [(features, i * span, span) for i in sets]))
    block_rows = [{0: [own[i]]} for i in sets]
    for i in sets:
        if groups == 4:
            block_rows[i][1] = [exchange(own[i], "grp", 1)]
            block_rows[i][2] = [exchange(own[i], "grp", 2)]
        else:
            mask = 1
            while mask < groups:
                for block in range(mask):
                    block_rows[i][block ^ mask] = [exchange(block_rows[i][block][0], "grp", mask)]
                mask *= 2

    def send_corner(i):
        (first,), (second,) = block_rows[i][1], block_rows[i][2]
        half = span // 2
        low, high = ran(copy_rows(turn(first, second), [(first, 0, half), (second, half, half)]))
        block_rows[i][3] = [exchange(low, "grp", 2), exchange(high, "grp", 1)]

    def multiply(pieces):
        rows = [block_rows[i][block] for i, block in pieces]
        keep, send = ran(
            forward(turn(*[part for parts in rows for part in parts]), rows, weight_here, slots)
        )
        return keep, send

    def add_pair(*events):
        events = [(keep, exchange(after(send, *last), "tp", 1)) for keep, send in events]
        own_sum, out = ran(sum_pair(turn(*[arrived for _, arrived in events]), events))
        return own_sum, [exchange(value, "tp", 2 * k) for k, value in enumerate(out, 1)]

    def add_planes(own_sum, arrived):
        return ran(sum_planes(turn(*arrived), own_sum, arrived))

    def add_rows(early, own_sum, arrived):
        hidden, part = ran(sum_rows(turn(*arrived), early, own_sum, arrived, gain, targets))
        return hidden, [part] + [exchange(part, "grp", mask) for mask in range(1, groups)]

    def differentiate(hidden, sums):
        return ran(gradient(turn(*sums), hidden, sums, gain, targets, share, all_units))

    def spread(grad, *waits):
        grad = after(grad, *waits)
        return [grad] + [exchange(grad, "tp", 2 * k) for k in range(1, slots)]

    def spread_pair(pieces, *waits):
        return pieces + [exchange(after(value, *waits), "tp", 1) for value in pieces]

    weight_here = load(turn(), weight)
    targets = ran(take_targets(turn(share), target, group_rows, len(sets), groups))
    own_pair = multiply([(i, 0) for i in sets])
    own_planes = add_pair(own_pair)
    if groups == 4 and len(sets) == 2:
        send_corner(0)
        edge0 = multiply([(0, 1), (0, 2)])
        own_hidden = add_planes(*own_planes)
        edge0 = add_pair(edge0)
        send_corner(1)
        edge1 = multiply([(1, 1), (1, 2)])
        hidden0 = add_planes(*edge0)
        edge1 = add_pair(edge1)
        corner0 = multiply([(0, 3)])
        corner1 = multiply([(1, 3)])
        hidden1 = add_planes(*edge1)
        early = [
            (own_hidden, 0, ROWS),
            (hidden0, 0, 2 * ROWS),
            (None, 0, ROWS),
            (own_hidden, ROWS, ROWS),
            (hidden1, 0, 2 * ROWS),
            (None, ROWS, ROWS),
        ]
        rows = add_rows(early, *add_pair(corner0, corner1))
    else:
        own_hidden = add_planes(*own_planes)
        early = []
        for i in sets:
            early.append((own_hidden, i * ROWS, ROWS))
            for block in range(1, groups):
                pair = add_pair(multiply([(i, block)]))
                if (i, block) != (sets[-1], groups - 1):
                    early.append((add_planes(*pair), 0, ROWS))
        rows = add_rows(early + [(None, 0, ROWS)], *pair)
    grads = differentiate(*rows)
    parts = [part for i in sets for block in range(groups) for part in block_rows[i][block]]
    planes = []
    for grad in grads:
        planes.append(spread(grad, *[pieces[1] for pieces in planes[-1:]]))
    result = loss = None
    for i, pieces in enumerate(planes):
        pieces = spread_pair(pieces, *([] if i == 0 else [loss]))
        result, total = backward(turn(*pieces), parts, pieces, i, gain.shape[1], result)
        loss = total if i == 0 else loss
        ran(loss)
    return (result, loss.reshape(()))


def solution(mesh):
    placed = (P("grp", "tp"), P("tp", "grp"), P("grp"), P(None, "grp"), P())
    return jax.shard_map(
        shards, mesh=mesh, in_specs=placed, out_specs=(P("tp", "grp"), P()), check_vma=False
    )
```
